512 devices in a mesh: win: 64 (over y, x, core), pair: 8 (over z).
Axes of the slice: x: 4, y: 8, z: 8, core: 2. Of those that a mesh axis runs over, the one named last changes fastest.
Arguments:
- spectra: float32 [128, 8, 64, 4096], P('win', 'pair'), may hold values from -6 to 6
- counts: int32 [64, 8], P('win', 'pair'), may hold values from 1 to 2
- band_filter: float32 [2048], replicated, may hold values from 0.1 to 1
- pair_list: int32 [8, 6, 2], P('pair'), may hold values from 0 to 7, as said below
- live_slots: int32 [8], P('pair'), may hold values from 1 to 6, as said below
Outputs:
- correlations: float32 [2048, 3072], P('win', 'pair')
The draws below stay inside these ranges and needn't reach their ends.
Inputs may be any that keep to these rules, and one draw needn't show every extreme that they name: `pair_list`: slot entries (a, b) of owner p satisfy a <= b, p - 1 <= a and b <= p + 1. `live_slots`: some owner uses all 6 slots.
All inputs are finite; a program needn't handle non-finite values.
Results may differ from the reference program's by a relative error of at most 0.0011.
Values sent between devices are 32-bit elements; how exact they have to be, the bound alone decides.
A program may use at most 64 MiB of HBM per device.

```python
import math
import jax
import jax.numpy as jnp
from jax import lax

CHANNELS = 64
BINS = 2048
LAGS = 2048
WIN_DEV = 2
SLOTS = 6
BLOCKS = 8
WINDOWS = 128
N_WIN = 64


def draw_pair_list(key, part):
    key = jax.random.fold_in(key, 11)
    lower = jnp.array([-1, -1, -1, 0, 0, 1], dtype=jnp.int32)
    upper = jnp.array([-1, 0, 1, 0, 1, 1], dtype=jnp.int32)
    choose = jax.random.randint(key, (BLOCKS, SLOTS), 0, 6)
    owners = jnp.arange(BLOCKS, dtype=jnp.int32)[:, None]
    first_block = jnp.clip(owners + lower[choose], 0, BLOCKS - 1)
    second_block = jnp.clip(owners + upper[choose], 0, BLOCKS - 1)
    slot_ids = jnp.arange(SLOTS, dtype=jnp.int32)[None, :]
    first_corner = (owners == 0) & (slot_ids == 0)
    last_corner = (owners == BLOCKS - 1) & (slot_ids == 0)
    first_block = jnp.where(first_corner, 0, jnp.where(last_corner, BLOCKS - 1, first_block))
    second_block = jnp.where(first_corner, 0, jnp.where(last_corner, BLOCKS - 1, second_block))
    return jnp.stack([first_block, second_block], axis=-1).astype(jnp.int32)


def draw_live_slots(key, part):
    key = jax.random.fold_in(key, 12)
    key_heavy, key_light, key_full = jax.random.split(key, 3)
    heavy = jax.random.randint(key_heavy, (BLOCKS,), 0, 3)
    light = jax.random.randint(key_light, (BLOCKS,), 1, SLOTS // 2 + 1)
    live_count = jnp.where(heavy == 0, SLOTS, light)
    chosen = jax.random.randint(key_full, (), 0, BLOCKS)
    live_count = jnp.where(jnp.arange(BLOCKS, dtype=jnp.int32) == chosen, SLOTS, live_count)
    return live_count.astype(jnp.int32)


def touch_ends(entries, stream_key, low, top_value):
    index_at = [jax.random.randint(jax.random.fold_in(stream_key, axis), (), 0, length) for axis, length in enumerate(entries.shape)]
    main_axis = entries.shape.index(max(entries.shape))
    neighbour = index_at[:main_axis] + [(index_at[main_axis] + 1) % entries.shape[main_axis]] + index_at[main_axis + 1:]
    return entries.at[tuple(index_at)].set(low).at[tuple(neighbour)].set(top_value)


def level_of(key, extent, shards, least, high):
    factor_of = 1.0
    for axis_at, shards_of in shards:
        heights = jax.random.uniform(jax.random.fold_in(jax.random.fold_in(key, 6), axis_at), (shards_of,), jnp.float32, least / len(shards), high / len(shards))
        factor_of = factor_of * jnp.repeat(jnp.exp(heights), extent[axis_at] // shards_of).reshape((-1,) + (1,) * (len(extent) - 1 - axis_at))
    return factor_of


def noise(key, extent, deviation, bound, pieces=(), kind=jnp.bfloat16):
    level = level_of(key, extent, pieces, -0.22, 0.18) if pieces else 1.0
    entries = jax.random.normal(key, extent, jnp.float32) * deviation * level
    return jnp.minimum(jnp.maximum(entries, -bound), bound).astype(kind)


def setup_inputs(seed: int = 0) -> dict:
    seeds = jax.random.split(jax.random.key(seed), 6)
    return {
        "spectra": noise(seeds[0], (WINDOWS, BLOCKS, CHANNELS, 2 * BINS), 1.0, 6.0, ((0, 64), (1, 8)), jnp.float32),
        "counts": touch_ends(jax.random.randint(seeds[1], (N_WIN, BLOCKS), 1, WIN_DEV + 1), jax.random.fold_in(seeds[1], 1), 1, WIN_DEV).astype(jnp.int32),
        "band_filter": jnp.clip(jnp.exp(jax.random.uniform(seeds[2], (BINS,), jnp.float32, math.log(0.1), math.log(1.0))), 0.1, 1.0),
        "pair_list": draw_pair_list(jax.random.fold_in(seeds[5], 71), 0),
        "live_slots": draw_live_slots(jax.random.fold_in(seeds[5], 71), 0),
    }


def whiten(spectra):
    return spectra * lax.rsqrt(lax.optimization_barrier(jnp.mean(spectra * spectra, axis=-1, keepdims=True)) + 1e-06)

def build_table():
    lag_values = jnp.arange(LAGS, dtype=jnp.int32) - LAGS // 2
    columns = jnp.arange(2 * BINS, dtype=jnp.int32)
    frequency = columns % BINS
    phase_angle = jnp.mod(lag_values[:, None] * frequency[None, :], 2 * BINS).astype(jnp.float32) * (math.pi / BINS)
    lag_table = jnp.where(columns[None, :] < BINS, jnp.cos(phase_angle), -jnp.sin(phase_angle)) * math.sqrt(2.0 / BINS)
    return lax.optimization_barrier(lag_table.astype(jnp.bfloat16)).astype(jnp.float32)

def reference(spectra, counts, band_filter, pair_list, live_slots):
    whitened = whiten(spectra).reshape(N_WIN, WIN_DEV, BLOCKS, CHANNELS, 2 * BINS)
    weight = jnp.concatenate([band_filter, band_filter])
    lag_table = build_table()
    windows = jnp.arange(WIN_DEV, dtype=jnp.float32)

    def one_owner(owner):
        slot_table = pair_list[owner]

        def one_slot(slot_index):
            first_block = slot_table[slot_index, 0]
            second_block = slot_table[slot_index, 1]
            left_spec = lax.dynamic_index_in_dim(whitened, first_block, 2, keepdims=False)
            right_spec = lax.dynamic_index_in_dim(whitened, second_block, 2, keepdims=False)
            kept_count = jnp.minimum(counts[:, first_block], counts[:, second_block])
            window_mask = (windows[None, :] < kept_count[:, None].astype(jnp.float32)).astype(jnp.float32)[:, :, None, None]
            left_real, left_imag = (left_spec[..., :BINS], left_spec[..., BINS:])
            right_real, right_imag = (right_spec[..., :BINS], right_spec[..., BINS:])
            real_part = lax.optimization_barrier(jnp.sum(window_mask * (left_real * right_real + left_imag * right_imag), axis=1))
            imag_part = lax.optimization_barrier(jnp.sum(window_mask * (left_imag * right_real - left_real * right_imag), axis=1))
            alive_flag = (slot_index < live_slots[owner]).astype(jnp.float32)
            stacked = (jnp.concatenate([real_part, imag_part], axis=-1) * weight * alive_flag).astype(jnp.bfloat16)
            summed = lax.optimization_barrier(jnp.sum(lax.optimization_barrier(stacked).astype(jnp.float32), axis=0))
            return (summed, jnp.sum(kept_count).astype(jnp.float32))
        stacks, totals = lax.map(one_slot, jnp.arange(SLOTS, dtype=jnp.int32))
        stack_rows = stacks.reshape(SLOTS * CHANNELS, 2 * BINS)
        term = jnp.dot(lag_table, stack_rows.T, precision=lax.Precision.HIGHEST, preferred_element_type=jnp.float32)
        return term / jnp.repeat(totals, CHANNELS)[None, :]
    per_owner = lax.map(one_owner, jnp.arange(BLOCKS, dtype=jnp.int32))
    return jnp.transpose(per_owner, (1, 0, 2)).reshape(LAGS, BLOCKS * SLOTS * CHANNELS)
```

```python
import math

import jax
import jax.numpy as jnp
import numpy as np
from jax import lax
from jax.experimental import pallas as pl
from jax.experimental.pallas import tpu as pltpu
from jax.sharding import PartitionSpec as P

LAGS = 2048
BINS = 2048
CHANNELS = 64
SLOTS = 6
ROWS = 8
PARTS = CHANNELS // ROWS
GROUP = 8
RING = 8
SHARE = LAGS // (GROUP * RING)
PIECE = SHARE * RING
HALF = PIECE // 2
KINDS = 3
LINES = KINDS * ROWS
AHEAD = 3
MESH = pl.DeviceIdType.MESH


def twiddles():
    frequency = np.arange(BINS, dtype=np.int64)[:, None]
    member = np.arange(2 * GROUP, dtype=np.int64)
    start = (member // 2) * SHARE + (member % 2) * (LAGS // 2) - LAGS // 2
    lane = np.arange(HALF, dtype=np.int64)
    place = (lane // SHARE) * PIECE + lane % SHARE

    def wave(offsets):
        angle = np.mod(frequency * offsets[None, :], 2 * BINS) * (math.pi / BINS)
        return np.cos(angle), np.sin(angle)

    start_cos, start_sin = wave(start)
    scale = math.sqrt(2.0 / BINS)
    place_cos, place_sin = wave(place)
    starts = np.zeros((BINS, 128), np.float32)
    starts[:, : 2 * GROUP] = start_cos
    starts[:, 2 * GROUP : 4 * GROUP] = start_sin
    places = np.concatenate([place_cos, place_sin], axis=1) * scale
    return starts, places.astype(np.float32)


def inverse_root(value):
    root = lax.rsqrt(value)
    return root * (1.5 - 0.5 * value * root * root)


def kernel(
    spectra, counts, band, pair_list, live, starts, places, out,
    own, low, high, first, second, table, stack, term, got_one, part, got_two, total,
    got_low, got_high, chosen, turned,
    count_own, count_low, count_high, kept, kept_one, kept_part, kept_two, kept_all, kept_low, kept_high,
    load_sem, halo_send, halo_recv, one_send, one_recv, two_send, two_recv, z_send, z_recv,
    count_send, count_recv, kept_one_send, kept_one_recv, kept_two_send, kept_two_recv, kept_z_send, kept_z_recv,
):
    win = lax.axis_index("win")
    plane = lax.axis_index("pair")
    row = win // GROUP
    member = win % GROUP
    above = (win, (plane + 1) % RING)
    below = (win, (plane + RING - 1) % RING)

    def in_group(step):
        return (row * GROUP + (member + step) % GROUP, plane)

    def in_ring(step):
        return (((row + step) % RING) * GROUP + member, plane)

    loads = [
        pltpu.make_async_copy(spectra.at[:, 0], own, load_sem.at[0]),
        pltpu.make_async_copy(starts, first, load_sem.at[1]),
        pltpu.make_async_copy(places, second, load_sem.at[2]),
    ]
    for load in loads:
        load.start()

    barrier = pltpu.get_barrier_semaphore()
    for neighbour in (above, below):
        pl.semaphore_signal(barrier, inc=1, device_id=neighbour, device_id_type=MESH)
    for step in range(1, GROUP):
        pl.semaphore_signal(barrier, inc=1, device_id=in_group(step), device_id_type=MESH)
    for step in range(1, RING):
        pl.semaphore_signal(barrier, inc=1, device_id=in_ring(step), device_id_type=MESH)
    count_own[...] = jnp.full((8, 128), counts[0, 0].astype(jnp.float32))
    pl.semaphore_wait(barrier, 2 + GROUP - 1 + RING - 1)

    def remote(source, target, send, recv, device):
        return pltpu.make_async_remote_copy(
            src_ref=source, dst_ref=target, send_sem=send, recv_sem=recv, device_id=device, device_id_type=MESH
        )

    def halo(index):
        block = spectra.at[:, 0, pl.ds(pl.multiple_of(index * ROWS, ROWS), ROWS), :]
        return (
            remote(block, low.at[index], halo_send.at[0, index], halo_recv.at[0, index], above),
            remote(block, high.at[index], halo_send.at[1, index], halo_recv.at[1, index], below),
        )

    count_copies = (
        remote(count_own, count_low, count_send.at[0], count_recv.at[0], above),
        remote(count_own, count_high, count_send.at[1], count_recv.at[1], below),
    )
    for copy in count_copies:
        copy.start()
    for index in range(AHEAD):
        for copy in halo(index):
            copy.start()

    loads[1].wait()
    loads[2].wait()
    stack[pl.ds(2 * 16 - 16, 16), :] = jnp.zeros((16, 2 * BINS), jnp.bfloat16)

    @pl.loop(0, BINS // 16)
    def _(block):
        rows = pl.ds(pl.multiple_of(block * 16, 16), 16)
        shifted = pl.ds(pl.multiple_of(block * 16 + BINS, 16), 16)
        place_cos = second[rows, 0:HALF]
        place_sin = second[rows, HALF : 2 * HALF]
        start_all = first[rows, :]
        for index in range(2 * GROUP):
            start_cos = start_all[:, index : index + 1]
            start_sin = start_all[:, 2 * GROUP + index : 2 * GROUP + index + 1]
            lanes = slice((index % 2) * HALF, (index % 2 + 1) * HALF)
            table[index // 2, rows, lanes] = (start_cos * place_cos - start_sin * place_sin).astype(jnp.bfloat16)
            table[index // 2, shifted, lanes] = (-(start_sin * place_cos) - start_cos * place_sin).astype(
                jnp.bfloat16
            )

    for copy in count_copies:
        copy.wait()
    mine = count_own[...]
    above_count = count_high[...]
    side = jnp.minimum(mine, above_count)
    across = jnp.minimum(count_low[...], above_count)
    line = lax.broadcasted_iota(jnp.int32, (8, 128), 0)
    kept[...] = jnp.where(line == 0, mine, jnp.where(line == 1, side, across))
    for step in range(1, GROUP):
        remote(kept, kept_one.at[step - 1], kept_one_send, kept_one_recv, in_group(step)).start()

    loads[0].wait()
    mask_own = jnp.where(mine > 1.5, 1.0, 0.0)
    mask_side = jnp.where(side > 1.5, 1.0, 0.0)
    mask_across = jnp.where(across > 1.5, 1.0, 0.0)

    def whole(ref, send, recv):
        return remote(ref, ref, send, recv, above)

    def correlate(index):
        for copy in halo(index):
            copy.wait_recv()

        @pl.when(index + AHEAD < PARTS)
        def _():
            for copy in halo(index + AHEAD):
                copy.start()

        here = pl.ds(pl.multiple_of(index * ROWS, ROWS), ROWS)

        def level(read):
            square = jnp.zeros((ROWS, 128), jnp.float32)
            for lane in range(0, 2 * BINS, 128):
                entry = read(slice(lane, lane + 128))
                square = square + entry * entry
            mean = jnp.sum(square, axis=1, keepdims=True) * (1.0 / (2 * BINS))
            return jnp.broadcast_to(inverse_root(mean + 1e-6), (ROWS, 128))

        def reader(kind, window):
            if kind == 0:
                return lambda lanes: own[window, here, lanes]
            ref = low if kind == 1 else high
            return lambda lanes: ref[index, window, :, lanes]

        readers = {(kind, window): reader(kind, window) for kind in range(3) for window in range(2)}
        levels = {key: level(read) for key, read in readers.items()}
        for lane in range(0, BINS, 128):
            real, imag = slice(lane, lane + 128), slice(BINS + lane, BINS + lane + 128)
            weight = jnp.broadcast_to(band[:, real], (ROWS, 128))
            re = {key: read(real) * levels[key] for key, read in readers.items()}
            im = {key: read(imag) * levels[key] for key, read in readers.items()}

            def cross(a, b, mask):
                parts = []
                for window in range(2):
                    ra, ia, rb, ib = re[a, window], im[a, window], re[b, window], im[b, window]
                    parts.append((ra * rb + ia * ib, ia * rb - ra * ib))
                return (
                    (parts[0][0] + mask * parts[1][0]) * weight,
                    (parts[0][1] + mask * parts[1][1]) * weight,
                )

            power = (re[0, 0] * re[0, 0] + im[0, 0] * im[0, 0]) + mask_own * (
                re[0, 1] * re[0, 1] + im[0, 1] * im[0, 1]
            )
            side_re, side_im = cross(0, 2, mask_side)
            across_re, across_im = cross(1, 2, mask_across)
            zero = jnp.zeros_like(power)
            stack[0:16, real] = jnp.concatenate([power * weight, side_re], axis=0).astype(jnp.bfloat16)
            stack[0:16, imag] = jnp.concatenate([zero, side_im], axis=0).astype(jnp.bfloat16)
            stack[16:32, real] = jnp.concatenate([across_re, zero], axis=0).astype(jnp.bfloat16)
            stack[16:32, imag] = jnp.concatenate([across_im, zero], axis=0).astype(jnp.bfloat16)

        def piece(step):
            product = lax.dot_general(
                stack[...],
                table[(member + step) % GROUP],
                (((1,), (0,)), ((), ())),
                preferred_element_type=jnp.float32,
            )
            term[index, step] = product[:LINES]

        @pl.loop(1, GROUP)
        def _(step):
            piece(step)
            remote(
                term.at[index, step], got_one.at[index, step - 1], one_send.at[index], one_recv.at[index], in_group(step)
            ).start()

        piece(0)

    def add_group(index):
        whole(got_one.at[index], one_send.at[index], one_recv.at[index]).wait_recv()
        for half in range(2):
            lanes = slice(half * HALF, (half + 1) * HALF)
            value = term[index, 0, :, lanes]
            for step in range(GROUP - 1):
                value = value + got_one[index, step, :, lanes]
            part[index, half] = value
        for step in range(1, RING):
            target = (row + step) % RING
            remote(
                part.at[index, target // (RING // 2)], got_two.at[index, step - 1],
                two_send.at[index], two_recv.at[index], in_ring(step),
            ).start()

    def z_copies(index):
        return (
            remote(total.at[index, pl.ds(0, 16)], got_low.at[index], z_send.at[0, index], z_recv.at[0, index], above),
            remote(total.at[index, pl.ds(0, 8)], got_high.at[index], z_send.at[1, index], z_recv.at[1, index], below),
        )

    def add_ring(index):
        whole(got_two.at[index], two_send.at[index], two_recv.at[index]).wait_recv()
        value = part[index, row // (RING // 2)]
        for step in range(RING - 1):
            value = value + got_two[index, step]
        total[index] = value
        for copy in z_copies(index):
            copy.start()

    def choose(options, slot):
        a, b = pair_list[0, slot, 0], pair_list[0, slot, 1]
        value = options[0]
        value = jnp.where((a == plane - 1) & (b == plane), options[1], value)
        value = jnp.where((a == plane - 1) & (b == plane + 1), options[2], value)
        value = jnp.where((a == plane) & (b == plane), options[3], value)
        value = jnp.where((a == plane) & (b == plane + 1), options[4], value)
        return jnp.where((a == plane + 1) & (b == plane + 1), options[5], value)

    def place_slots(index):
        for copy in z_copies(index):
            copy.wait()
        whole(term.at[index, pl.ds(1, GROUP - 1)], one_send.at[index], one_recv.at[index]).wait_send()
        whole(got_two.at[index], two_send.at[index], two_recv.at[index]).wait_send()
        for copy in halo(index):
            copy.wait_send()
        options = [
            got_low[index, 0:8], got_low[index, 8:16], total[index, 16:24],
            total[index, 0:8], total[index, 8:16], got_high[index],
        ]
        for slot in range(SLOTS):
            chosen[pl.ds(pl.multiple_of(slot * CHANNELS + index * ROWS, ROWS), ROWS), :] = choose(options, slot)

    def kept_copies():
        return (
            remote(kept_all, kept_low, kept_z_send.at[0], kept_z_recv.at[0], above),
            remote(kept_all, kept_high, kept_z_send.at[1], kept_z_recv.at[1], below),
        )

    @pl.loop(0, PARTS + 3)
    def _(turn):
        @pl.when(turn < PARTS)
        def _():
            correlate(turn)

        @pl.when((turn >= 1) & (turn < PARTS + 1))
        def _():
            add_group(turn - 1)

        @pl.when(turn == 1)
        def _():
            whole(kept_one, kept_one_send, kept_one_recv).wait()
            value = kept[...]
            for step in range(GROUP - 1):
                value = value + kept_one[step]
            kept_part[...] = value
            for step in range(1, RING):
                remote(kept_part, kept_two.at[step - 1], kept_two_send, kept_two_recv, in_ring(step)).start()

        @pl.when((turn >= 2) & (turn < PARTS + 2))
        def _():
            add_ring(turn - 2)

        @pl.when(turn == 3)
        def _():
            whole(kept_two, kept_two_send, kept_two_recv).wait()
            value = kept_part[...]
            for step in range(RING - 1):
                value = value + kept_two[step]
            kept_all[...] = value
            for copy in kept_copies():
                copy.start()

        @pl.when(turn == 5)
        def _():
            for copy in kept_copies():
                copy.wait()

        @pl.when(turn >= 3)
        def _():
            place_slots(turn - 3)

    kept_options = [
        kept_low[0:1], kept_low[1:2], kept_all[2:3], kept_all[0:1], kept_all[1:2], kept_high[0:1],
    ]
    for slot in range(SLOTS):
        alive = (slot < live[0]).astype(jnp.float32)
        scale = alive / choose(kept_options, slot)
        rows = slice(slot * CHANNELS, (slot + 1) * CHANNELS)
        chosen[rows, :] = chosen[rows, :] * scale
    for block in range(SLOTS * CHANNELS // 128):
        turned[:, block * 128 : (block + 1) * 128] = chosen[block * 128 : (block + 1) * 128, :].T
    out[...] = turned[pl.ds(pl.multiple_of((row % (RING // 2)) * SHARE, SHARE), SHARE), :]


def on_device(spectra, counts, band_filter, pair_list, live_slots):
    starts, places = twiddles()
    f32 = jnp.float32
    dma = pltpu.SemaphoreType.DMA
    tile = (8, 128)
    return pl.pallas_call(
        kernel,
        out_shape=jax.ShapeDtypeStruct((SHARE, SLOTS * CHANNELS), f32),
        in_specs=[
            pl.BlockSpec(memory_space=pl.ANY),
            pl.BlockSpec(memory_space=pltpu.SMEM),
            pl.BlockSpec(memory_space=pltpu.VMEM),
            pl.BlockSpec(memory_space=pltpu.SMEM),
            pl.BlockSpec(memory_space=pltpu.SMEM),
            pl.BlockSpec(memory_space=pl.ANY),
            pl.BlockSpec(memory_space=pl.ANY),
        ],
        out_specs=pl.BlockSpec(memory_space=pltpu.VMEM),
        scratch_shapes=[
            pltpu.VMEM((2, CHANNELS, 2 * BINS), f32),
            pltpu.VMEM((PARTS, 2, ROWS, 2 * BINS), f32),
            pltpu.VMEM((PARTS, 2, ROWS, 2 * BINS), f32),
            pltpu.VMEM((BINS, 128), f32),
            pltpu.VMEM((BINS, 2 * HALF), f32),
            pltpu.VMEM((GROUP, 2 * BINS, PIECE), jnp.bfloat16),
            pltpu.VMEM((32, 2 * BINS), jnp.bfloat16),
            pltpu.VMEM((PARTS, GROUP, LINES, PIECE), f32),
            pltpu.VMEM((PARTS, GROUP - 1, LINES, PIECE), f32),
            pltpu.VMEM((PARTS, 2, LINES, HALF), f32),
            pltpu.VMEM((PARTS, RING - 1, LINES, HALF), f32),
            pltpu.VMEM((PARTS, LINES, HALF), f32),
            pltpu.VMEM((PARTS, 2 * ROWS, HALF), f32),
            pltpu.VMEM((PARTS, ROWS, HALF), f32),
            pltpu.VMEM((SLOTS * CHANNELS, HALF), f32),
            pltpu.VMEM((HALF, SLOTS * CHANNELS), f32),
            pltpu.VMEM(tile, f32),
            pltpu.VMEM(tile, f32),
            pltpu.VMEM(tile, f32),
            pltpu.VMEM(tile, f32),
            pltpu.VMEM((GROUP - 1,) + tile, f32),
            pltpu.VMEM(tile, f32),
            pltpu.VMEM((RING - 1,) + tile, f32),
            pltpu.VMEM(tile, f32),
            pltpu.VMEM(tile, f32),
            pltpu.VMEM(tile, f32),
            dma((3,)),
            dma((2, PARTS)), dma((2, PARTS)),
            dma((PARTS,)), dma((PARTS,)),
            dma((PARTS,)), dma((PARTS,)),
            dma((2, PARTS)), dma((2, PARTS)),
            dma((2,)), dma((2,)),
            dma, dma, dma, dma,
            dma((2,)), dma((2,)),
        ],
        compiler_params=pltpu.CompilerParams(
            collective_id=0, has_side_effects=True, vmem_limit_bytes=56 * 1024 * 1024
        ),
    )(spectra, counts, band_filter.reshape(1, BINS), pair_list, live_slots, jnp.asarray(starts), jnp.asarray(places))


def solution(mesh):
    placed = (P("win", "pair", None, None), P("win", "pair"), P(), P("pair", None, None), P("pair"))
    return jax.shard_map(
        on_device, mesh=mesh, in_specs=placed, out_specs=P("win", "pair"), check_vma=False
    )
```

```python
import math

import jax
import jax.numpy as jnp
import numpy as np
from jax import lax
from jax.experimental import pallas as pl
from jax.experimental.pallas import tpu as pltpu
from jax.sharding import PartitionSpec as P

LAGS = 2048
BINS = 2048
CHANNELS = 64
SLOTS = 6
ROWS = 8
PARTS = CHANNELS // ROWS
GROUP = 8
RING = 8
SHARE = LAGS // (GROUP * RING)
PIECE = SHARE * RING
HALF = PIECE // 2
LINES = 2 * ROWS
AHEAD = 3
MESH = pl.DeviceIdType.MESH


def twiddles():
    frequency = np.arange(BINS, dtype=np.int64)[:, None]
    lane = np.arange(HALF, dtype=np.int64)
    place = (lane // SHARE) * PIECE + lane % SHARE

    def wave(offsets):
        angle = np.mod(frequency * offsets[None, :], 2 * BINS) * (math.pi / BINS)
        return np.cos(angle), np.sin(angle)

    turns = np.zeros((BINS, 128), np.float32)
    turn_cos, turn_sin = wave(np.array([SHARE], np.int64))
    turns[:, 0:1], turns[:, 1:2] = turn_cos, turn_sin
    place_cos, place_sin = wave(place)
    places = np.concatenate([place_cos, -place_sin], axis=1) * math.sqrt(2.0 / BINS)
    return turns, places.astype(np.float32)


def inverse_root(value):
    root = lax.rsqrt(value)
    return root * (1.5 - 0.5 * value * root * root)


def kernel(
    spectra, counts_hbm, band, pairs_hbm, live_hbm, turns, places, out,
    counts, pairs, live,
    own, own_level, low, high, turn_table, place_table, table,
    own_stack, own_term, own_got_one, own_pack, own_got_two, own_total, own_low, own_high, own_wide,
    stack, term, got_one, pack, got_two, total, got_low, chosen,
    count_own, count_low, count_high, kept, kept_one, kept_part, kept_two, kept_all, kept_low, kept_high,
    load_sem, halo_send, halo_recv, one_send, one_recv, two_send, two_recv, z_send, z_recv,
    own_one_send, own_one_recv, own_two_send, own_two_recv, own_z_send, own_z_recv,
    count_send, count_recv, kept_one_send, kept_one_recv, kept_two_send, kept_two_recv, kept_z_send, kept_z_recv,
):
    win = lax.axis_index("win")
    plane = lax.axis_index("pair")
    row = win // GROUP
    member = win % GROUP
    above = (win, (plane + 1) % RING)
    below = (win, (plane + RING - 1) % RING)

    def in_group(step):
        return (row * GROUP + (member + step) % GROUP, plane)

    def in_ring(step):
        return (((row + step) % RING) * GROUP + member, plane)

    barrier = pltpu.get_barrier_semaphore()
    for neighbour in (above, below):
        pl.semaphore_signal(barrier, inc=1, device_id=neighbour, device_id_type=MESH)
    for step in range(1, GROUP):
        pl.semaphore_signal(barrier, inc=1, device_id=in_group(step), device_id_type=MESH)
    for step in range(1, RING):
        pl.semaphore_signal(barrier, inc=1, device_id=in_ring(step), device_id_type=MESH)

    count_load = pltpu.make_async_copy(counts_hbm, counts, load_sem.at[0])
    pairs_load = pltpu.make_async_copy(pairs_hbm, pairs, load_sem.at[1])
    live_load = pltpu.make_async_copy(live_hbm, live, load_sem.at[2])
    turn_load = pltpu.make_async_copy(turns, turn_table, load_sem.at[3])
    place_load = pltpu.make_async_copy(places, place_table, load_sem.at[4])
    own_load = pltpu.make_async_copy(spectra.at[:, 0], own, load_sem.at[5])
    for load in (count_load, pairs_load, live_load, turn_load, place_load, own_load):
        load.start()
    count_load.wait()
    count_own[...] = jnp.full((8, 128), counts[0, 0].astype(jnp.float32))
    pl.semaphore_wait(barrier, 2 + GROUP - 1 + RING - 1)

    def remote(source, target, send, recv, device):
        return pltpu.make_async_remote_copy(
            src_ref=source, dst_ref=target, send_sem=send, recv_sem=recv, device_id=device, device_id_type=MESH
        )

    def whole(ref, send, recv):
        return remote(ref, ref, send, recv, above)

    def halo(index):
        block = spectra.at[:, 0, pl.ds(pl.multiple_of(index * ROWS, ROWS), ROWS), :]
        return (
            remote(block, low.at[index], halo_send.at[0, index], halo_recv.at[0, index], above),
            remote(block, high.at[index], halo_send.at[1, index], halo_recv.at[1, index], below),
        )

    def both_sides(source, to_above, to_below, send, recv):
        return (
            remote(source, to_above, send.at[0], recv.at[0], above),
            remote(source, to_below, send.at[1], recv.at[1], below),
        )

    count_copies = both_sides(count_own, count_low, count_high, count_send, count_recv)
    for copy in count_copies:
        copy.start()
    for index in range(AHEAD):
        for copy in halo(index):
            copy.start()

    turn_load.wait()
    place_load.wait()
    line = lax.broadcasted_iota(jnp.int32, (16, 128), 0)
    odd = (line % 2) == 1
    sign_sin = jnp.where(line % 4 < 2, 1.0, -1.0)
    sign_cos = jnp.where((line % 4 == 0) | (line % 4 == 3), 1.0, -1.0)

    @pl.loop(0, BINS // 16, unroll=2)
    def _(block):
        rows = pl.ds(pl.multiple_of(block * 16, 16), 16)
        shifted = pl.ds(pl.multiple_of(block * 16 + BINS, 16), 16)
        cos = place_table[rows, 0:HALF]
        minus_sin = place_table[rows, HALF : 2 * HALF]
        turn_cos = jnp.broadcast_to(turn_table[rows, 0:1], (16, 128))
        turn_sin = jnp.broadcast_to(turn_table[rows, 1:2], (16, 128))
        for index in range(GROUP):
            table[index, rows, HALF : 2 * HALF] = cos.astype(jnp.bfloat16)
            table[index, shifted, HALF : 2 * HALF] = minus_sin.astype(jnp.bfloat16)
            table[index, rows, 0:HALF] = (jnp.where(odd, minus_sin, cos) * sign_cos).astype(jnp.bfloat16)
            table[index, shifted, 0:HALF] = (jnp.where(odd, cos, minus_sin) * sign_sin).astype(jnp.bfloat16)
            if index < GROUP - 1:
                cos, minus_sin = (
                    cos * turn_cos + minus_sin * turn_sin,
                    minus_sin * turn_cos - cos * turn_sin,
                )

    def level(read, rows):
        square = jnp.zeros((rows, 128), jnp.float32)
        for lane in range(0, 2 * BINS, 128):
            entry = read(slice(lane, lane + 128))
            square = square + entry * entry
        mean = jnp.sum(square, axis=1, keepdims=True) * (1.0 / (2 * BINS))
        return jnp.broadcast_to(inverse_root(mean + 1e-6), (rows, 128))

    own_load.wait()
    mine = count_own[...]
    mask_own = jnp.concatenate([jnp.where(mine > 1.5, 1.0, 0.0)] * 2, axis=0)

    @pl.loop(0, CHANNELS // 16)
    def _(block):
        here = pl.ds(pl.multiple_of(block * 16, 16), 16)
        levels = []
        for window in range(2):
            levels.append(level(lambda lanes: own[window, here, lanes], 16))
            own_level[window, here, :] = levels[window]
        for lane in range(0, BINS, 128):
            real, imag = slice(lane, lane + 128), slice(BINS + lane, BINS + lane + 128)
            powers = []
            for window in range(2):
                re, im = own[window, here, real] * levels[window], own[window, here, imag] * levels[window]
                powers.append(re * re + im * im)
            weight = jnp.broadcast_to(band[:, real], (16, 128))
            own_stack[here, real] = ((powers[0] + mask_own * powers[1]) * weight).astype(jnp.bfloat16)

    def own_piece(step):
        own_term[step] = lax.dot_general(
            own_stack[...],
            table[(member + step) % GROUP, 0:BINS],
            (((1,), (0,)), ((), ())),
            preferred_element_type=jnp.float32,
        )

    @pl.loop(1, GROUP)
    def _(step):
        own_piece(step)
        remote(own_term.at[step], own_got_one.at[step - 1], own_one_send, own_one_recv, in_group(step)).start()

    own_piece(0)

    for copy in count_copies:
        copy.wait()
    above_count = count_high[...]
    side = jnp.minimum(mine, above_count)
    across = jnp.minimum(count_low[...], above_count)
    row_line = lax.broadcasted_iota(jnp.int32, (8, 128), 0)
    kept[...] = jnp.where(row_line == 0, mine, jnp.where(row_line == 1, side, across))
    for step in range(1, GROUP):
        remote(kept, kept_one.at[step - 1], kept_one_send, kept_one_recv, in_group(step)).start()
    mask_side = jnp.where(side > 1.5, 1.0, 0.0)
    mask_across = jnp.where(across > 1.5, 1.0, 0.0)

    def correlate(index):
        for copy in halo(index):
            copy.wait_recv()

        @pl.when(index + AHEAD < PARTS)
        def _():
            for copy in halo(index + AHEAD):
                copy.start()

        here = pl.ds(pl.multiple_of(index * ROWS, ROWS), ROWS)

        def reader(kind, window):
            if kind == 0:
                return lambda lanes: own[window, here, lanes]
            ref = low if kind == 1 else high
            return lambda lanes: ref[index, window, :, lanes]

        readers = {(kind, window): reader(kind, window) for kind in range(3) for window in range(2)}
        levels = {
            key: own_level[key[1], here, :] if key[0] == 0 else level(read, ROWS) for key, read in readers.items()
        }
        for lane in range(0, BINS, 128):
            real, imag = slice(lane, lane + 128), slice(BINS + lane, BINS + lane + 128)
            weight = jnp.broadcast_to(band[:, real], (ROWS, 128))
            re = {key: read(real) * levels[key] for key, read in readers.items()}
            im = {key: read(imag) * levels[key] for key, read in readers.items()}

            def cross(a, b, mask):
                parts = []
                for window in range(2):
                    ra, ia, rb, ib = re[a, window], im[a, window], re[b, window], im[b, window]
                    parts.append((ra * rb + ia * ib, ia * rb - ra * ib))
                return (
                    (parts[0][0] + mask * parts[1][0]) * weight,
                    (parts[0][1] + mask * parts[1][1]) * weight,
                )

            side_re, side_im = cross(0, 2, mask_side)
            across_re, across_im = cross(1, 2, mask_across)
            stack[:, real] = jnp.concatenate([side_re, across_re], axis=0).astype(jnp.bfloat16)
            stack[:, imag] = jnp.concatenate([side_im, across_im], axis=0).astype(jnp.bfloat16)

        def piece(step):
            term[index, step] = lax.dot_general(
                stack[...],
                table[(member + step) % GROUP],
                (((1,), (0,)), ((), ())),
                preferred_element_type=jnp.float32,
            )

        @pl.loop(1, GROUP)
        def _(step):
            piece(step)
            remote(
                term.at[index, step], got_one.at[index, step - 1], one_send.at[index], one_recv.at[index], in_group(step)
            ).start()

        piece(0)

    def packed(groups, chip):
        lane = lax.broadcasted_iota(jnp.int32, groups[0].shape, 1)
        value = None
        for place in reversed(range(len(groups))):
            shift = ((place - chip) * SHARE) % 128
            moved = pltpu.roll(groups[place], shift, axis=1) if shift else groups[place]
            value = moved if value is None else jnp.where(lane < (place + 1) * SHARE, moved, value)
        return value

    def add_group(index):
        whole(got_one.at[index], one_send.at[index], one_recv.at[index]).wait_recv()
        for half in range(2):
            lanes = slice(half * HALF, (half + 1) * HALF)
            value = term[index, 0, :, lanes]
            for step in range(GROUP - 1):
                value = value + got_one[index, step, :, lanes]
            for chip in range(RING // 2):
                pack[index, half * (RING // 2) + chip] = packed([value[:ROWS], value[ROWS:]], chip)
        for step in range(1, RING):
            remote(
                pack.at[index, (row + step) % RING], got_two.at[index, step - 1],
                two_send, two_recv.at[index], in_ring(step),
            ).start()

    def add_ring(index):
        whole(got_two.at[index], two_send, two_recv.at[index]).wait_recv()
        value = pack[index, row]
        for step in range(RING - 1):
            value = value + got_two[index, step]
        total[index] = value
        remote(total.at[index], got_low.at[index], z_send, z_recv, above).start()
        whole(got_one.at[index], one_send.at[index], one_recv.at[index]).wait_send()
        for copy in halo(index):
            copy.wait_send()

    @pl.loop(0, PARTS + 2)
    def _(turn):
        @pl.when(turn < PARTS)
        def _():
            correlate(turn)

        @pl.when((turn >= 1) & (turn < PARTS + 1))
        def _():
            add_group(turn - 1)

        @pl.when(turn >= 2)
        def _():
            add_ring(turn - 2)

        @pl.when(turn == 2)
        def _():
            whole(kept_one, kept_one_send, kept_one_recv).wait()
            value = kept[...]
            for step in range(GROUP - 1):
                value = value + kept_one[step]
            kept_part[...] = value
            whole(own_got_one, own_one_send, own_one_recv).wait()
            for half in range(2):
                lanes = slice(half * HALF, (half + 1) * HALF)
                groups = []
                for block in range(4):
                    rows = slice(block * 16, (block + 1) * 16)
                    value = own_term[0, rows, lanes]
                    for step in range(GROUP - 1):
                        value = value + own_got_one[step, rows, lanes]
                    groups.append(value)
                for chip in range(RING // 2):
                    own_pack[half * (RING // 2) + chip] = packed(groups, chip)
            for step in range(1, RING):
                remote(kept_part, kept_two.at[step - 1], kept_two_send, kept_two_recv, in_ring(step)).start()
                remote(
                    own_pack.at[(row + step) % RING], own_got_two.at[step - 1], own_two_send, own_two_recv, in_ring(step)
                ).start()

        @pl.when(turn == 4)
        def _():
            whole(kept_two, kept_two_send, kept_two_recv).wait()
            whole(own_got_two, own_two_send, own_two_recv).wait()
            value = kept_part[...]
            own_value = own_pack[row]
            for step in range(RING - 1):
                value = value + kept_two[step]
                own_value = own_value + own_got_two[step]
            kept_all[...] = value
            own_total[...] = own_value
            for copy in both_sides(kept_all, kept_low, kept_high, kept_z_send, kept_z_recv):
                copy.start()
            for copy in both_sides(own_total, own_low, own_high, own_z_send, own_z_recv):
                copy.start()

        @pl.when(turn == 6)
        def _():
            for copy in both_sides(kept_all, kept_low, kept_high, kept_z_send, kept_z_recv):
                copy.wait()
            for copy in both_sides(own_total, own_low, own_high, own_z_send, own_z_recv):
                copy.wait()
            for place, source in enumerate((own_low, own_total, own_high)):
                value = source[...]
                for block in range(4):
                    rows = slice(block * 16, (block + 1) * 16)
                    own_wide[place, rows, :] = pltpu.roll(value, 128 - block * SHARE, axis=1) if block else value

    pairs_load.wait()
    live_load.wait()
    whole(got_two, two_send, two_recv.at[0]).wait_send()
    whole(got_low, z_send, z_recv).wait()
    kept_options = [
        kept_low[0:1], kept_low[1:2], kept_all[2:3], kept_all[0:1], kept_all[1:2], kept_high[0:1],
    ]
    for slot in range(SLOTS):
        a, b = pairs[0, 0, slot], pairs[0, 1, slot]
        tests = [
            (a == plane - 1) & (b == plane),
            (a == plane - 1) & (b == plane + 1),
            (a == plane) & (b == plane),
            (a == plane) & (b == plane + 1),
            (a == plane + 1) & (b == plane + 1),
        ]

        def choose(options):
            value = options[0]
            for test, option in zip(tests, options[1:]):
                value = jnp.where(test, option, value)
            return value

        alive = (slot < live[0]).astype(jnp.float32)
        scale = jnp.broadcast_to(alive / choose(kept_options), (ROWS, 128))
        for index in range(PARTS):
            rows = slice(index * ROWS, (index + 1) * ROWS)
            value = choose([
                own_wide[0, rows], got_low[index], pltpu.roll(total[index], 128 - SHARE, axis=1),
                own_wide[1, rows], total[index], own_wide[2, rows],
            ])
            chosen[slot * CHANNELS + index * ROWS : slot * CHANNELS + (index + 1) * ROWS, :] = value * scale
    for block in range(SLOTS * CHANNELS // 128):
        lanes = slice(block * 128, (block + 1) * 128)
        out[:, lanes] = chosen[lanes, :].T[:SHARE]


def on_device(spectra, counts, band_filter, pair_list, live_slots):
    turns, places = twiddles()
    f32, bf16, i32 = jnp.float32, jnp.bfloat16, jnp.int32
    dma = pltpu.SemaphoreType.DMA
    tile = (8, 128)
    vmem = pltpu.VMEM
    anywhere = pl.BlockSpec(memory_space=pl.ANY)
    return pl.pallas_call(
        kernel,
        out_shape=jax.ShapeDtypeStruct((SHARE, SLOTS * CHANNELS), f32),
        in_specs=[anywhere, anywhere, pl.BlockSpec(memory_space=vmem), anywhere, anywhere, anywhere, anywhere],
        out_specs=pl.BlockSpec(memory_space=vmem),
        scratch_shapes=[
            pltpu.SMEM((1, 1), i32), pltpu.SMEM((1, 2, SLOTS), i32), pltpu.SMEM((1,), i32),
            vmem((2, CHANNELS, 2 * BINS), f32),
            vmem((2, CHANNELS, 128), f32),
            vmem((PARTS, 2, ROWS, 2 * BINS), f32),
            vmem((PARTS, 2, ROWS, 2 * BINS), f32),
            vmem((BINS, 128), f32),
            vmem((BINS, 2 * HALF), f32),
            vmem((GROUP, 2 * BINS, PIECE), bf16),
            vmem((CHANNELS, BINS), bf16),
            vmem((GROUP, CHANNELS, PIECE), f32),
            vmem((GROUP - 1, CHANNELS, PIECE), f32),
            vmem((RING, 16, 128), f32),
            vmem((RING - 1, 16, 128), f32),
            vmem((16, 128), f32), vmem((16, 128), f32), vmem((16, 128), f32),
            vmem((3, CHANNELS, 128), f32),
            vmem((LINES, 2 * BINS), bf16),
            vmem((PARTS, GROUP, LINES, PIECE), f32),
            vmem((PARTS, GROUP - 1, LINES, PIECE), f32),
            vmem((PARTS, RING) + tile, f32),
            vmem((PARTS, RING - 1) + tile, f32),
            vmem((PARTS,) + tile, f32),
            vmem((PARTS,) + tile, f32),
            vmem((SLOTS * CHANNELS, 128), f32),
            vmem(tile, f32), vmem(tile, f32), vmem(tile, f32),
            vmem(tile, f32),
            vmem((GROUP - 1,) + tile, f32),
            vmem(tile, f32),
            vmem((RING - 1,) + tile, f32),
            vmem(tile, f32), vmem(tile, f32), vmem(tile, f32),
            dma((6,)),
            dma((2, PARTS)), dma((2, PARTS)),
            dma((PARTS,)), dma((PARTS,)),
            dma, dma((PARTS,)),
            dma, dma,
            dma, dma, dma, dma,
            dma((2,)), dma((2,)),
            dma((2,)), dma((2,)),
            dma, dma, dma, dma,
            dma((2,)), dma((2,)),
        ],
        compiler_params=pltpu.CompilerParams(
            collective_id=0, has_side_effects=True, vmem_limit_bytes=56 * 1024 * 1024
        ),
    )(
        spectra, counts, band_filter.reshape(1, BINS), jnp.swapaxes(pair_list, 1, 2), live_slots,
        jnp.asarray(turns), jnp.asarray(places),
    )


def solution(mesh):
    placed = (P("win", "pair", None, None), P("win", "pair"), P(), P("pair", None, None), P("pair"))
    return jax.shard_map(
        on_device, mesh=mesh, in_specs=placed, out_specs=P("win", "pair"), check_vma=False
    )
```

```python
import math

import jax
import jax.numpy as jnp
import numpy as np
from jax import lax
from jax.experimental import pallas as pl
from jax.experimental.pallas import tpu as pltpu
from jax.sharding import PartitionSpec as P

LAGS = 2048
BINS = 2048
CHANNELS = 64
SLOTS = 6
ROWS = 8
PARTS = CHANNELS // ROWS
GROUP = 8
RING = 8
SHARE = LAGS // (GROUP * RING)
PIECE = SHARE * RING
HALF = PIECE // 2
LINES = 2 * ROWS
AHEAD = 2
LAST = PARTS - 1
RUNS = ((0, 1280), (1280, BINS))
PAIRS = 3
UNITS = PAIRS + 2
TAIL = PAIRS - 1
MESH = pl.DeviceIdType.MESH


def twiddles():
    frequency = np.arange(BINS, dtype=np.int64)[:, None]
    lane = np.arange(HALF, dtype=np.int64)
    place = (lane // SHARE) * PIECE + lane % SHARE

    def wave(offsets):
        angle = np.mod(frequency * offsets[None, :], 2 * BINS) * (math.pi / BINS)
        return np.cos(angle), np.sin(angle)

    turns = np.zeros((BINS, 128), np.float32)
    turn_cos, turn_sin = wave(np.array([SHARE], np.int64))
    turns[:, 0:1], turns[:, 1:2] = turn_cos, turn_sin
    place_cos, place_sin = wave(place)
    places = np.concatenate([place_cos, -place_sin], axis=1) * math.sqrt(2.0 / BINS)
    return turns, places.astype(np.float32)


def inverse_root(value):
    root = lax.rsqrt(value)
    return root * (1.5 - 0.5 * value * root * root)


def kernel(
    spectra, counts_hbm, band, pairs_hbm, live_hbm, turns, places, out,
    counts, pairs, live,
    own, own_level, low, high, turn_table, place_table, table,
    own_stack, own_term, own_got_one, own_pack, own_got_two, own_total, own_low, own_high, own_wide,
    stack, term, got_one, pack, got_two, got_two_low, total, got_low, chosen, level_low, level_high,
    count_own, count_low, count_high, kept, kept_one, kept_part, kept_two, kept_all, kept_low, kept_high,
    load_sem, halo_send, halo_recv, one_send, one_recv, two_send, two_recv, two_low_send, two_low_recv, z_send, z_recv,
    run_send, run_recv, level_send, level_recv,
    own_one_send, own_one_recv, own_two_send, own_two_recv, own_z_send, own_z_recv,
    count_send, count_recv, kept_one_send, kept_one_recv, kept_two_send, kept_two_recv, kept_z_send, kept_z_recv,
):
    win = lax.axis_index("win")
    plane = lax.axis_index("pair")
    row = win // GROUP
    member = win % GROUP
    above = (win, (plane + 1) % RING)
    below = (win, (plane + RING - 1) % RING)
    has_above, has_below = plane < RING - 1, plane > 0
    sends_up, takes_low = plane < RING - 2, (plane > 0) & (plane < RING - 1)
    sends_down, takes_high = plane > 0, plane < RING - 1

    def in_group(step):
        return (row * GROUP + (member + step) % GROUP, plane)

    def in_ring(step):
        return (((row + step) % RING) * GROUP + member, plane)

    for ref in (count_low, count_high, kept_low, kept_high):
        ref[...] = jnp.ones_like(ref)
    for ref in (own_low, own_high, got_low, level_low, level_high):
        ref[...] = jnp.zeros_like(ref)

    barrier = pltpu.get_barrier_semaphore()

    @pl.when(has_above)
    def _():
        pl.semaphore_signal(barrier, inc=1, device_id=above, device_id_type=MESH)

    @pl.when(has_below)
    def _():
        pl.semaphore_signal(barrier, inc=1, device_id=below, device_id_type=MESH)

    for step in range(1, GROUP):
        pl.semaphore_signal(barrier, inc=1, device_id=in_group(step), device_id_type=MESH)
    for step in range(1, RING):
        pl.semaphore_signal(barrier, inc=1, device_id=in_ring(step), device_id_type=MESH)

    count_load = pltpu.make_async_copy(counts_hbm, counts, load_sem.at[0])
    pairs_load = pltpu.make_async_copy(pairs_hbm, pairs, load_sem.at[1])
    live_load = pltpu.make_async_copy(live_hbm, live, load_sem.at[2])
    turn_load = pltpu.make_async_copy(turns, turn_table, load_sem.at[3])
    place_load = pltpu.make_async_copy(places, place_table, load_sem.at[4])
    own_load = pltpu.make_async_copy(spectra.at[:, 0], own, load_sem.at[5])
    for load in (count_load, pairs_load, live_load, turn_load, place_load, own_load):
        load.start()
    count_load.wait()
    count_own[...] = jnp.full((8, 128), counts[0, 0].astype(jnp.float32))
    pl.semaphore_wait(barrier, GROUP - 1 + RING - 1 + has_above.astype(jnp.int32) + has_below.astype(jnp.int32))

    def remote(source, target, send, recv, device):
        return pltpu.make_async_remote_copy(
            src_ref=source, dst_ref=target, send_sem=send, recv_sem=recv, device_id=device, device_id_type=MESH
        )

    def whole(ref, send, recv):
        return remote(ref, ref, send, recv, above)

    def both_sides(up, low_ref, down, high_ref, send, recv):
        return (
            remote(up, low_ref, send.at[0], recv.at[0], above),
            remote(down, high_ref, send.at[1], recv.at[1], below),
        )

    def halo(index):
        block = spectra.at[:, 0, pl.ds(pl.multiple_of(index * ROWS, ROWS), ROWS), :]
        return both_sides(block, low.at[index], block, high.at[index], halo_send.at[index], halo_recv.at[index])

    def runs(run):
        copies = []
        for side in range(2):
            lanes = pl.ds(side * BINS + RUNS[run][0], RUNS[run][1] - RUNS[run][0])
            block = spectra.at[:, 0, pl.ds(LAST * ROWS, ROWS), lanes]
            copies.append(
                both_sides(
                    block, low.at[LAST, :, :, lanes], block, high.at[LAST, :, :, lanes],
                    run_send.at[run, side], run_recv.at[run, side],
                )
            )
        return copies

    def next_halo(index):
        within = index < LAST
        begin(halo(lax.rem(index, PARTS)), sends_up & within, sends_down & within)
        for run in range(len(RUNS)):
            for copies in runs(run):
                begin(copies, sends_up & (index == LAST + run), sends_down & (index == LAST + run))

    def begin(copies, up, down):
        pl.when(up)(copies[0].start)
        pl.when(down)(copies[1].start)

    def end_send(copies, up, down):
        pl.when(up)(copies[0].wait_send)
        pl.when(down)(copies[1].wait_send)

    def end_recv(copies, takes_low, takes_high):
        pl.when(takes_low)(copies[0].wait_recv)
        pl.when(takes_high)(copies[1].wait_recv)

    for index in range(AHEAD):
        begin(halo(index), sends_up, sends_down)
    count_copies = both_sides(count_own, count_low, count_own, count_high, count_send, count_recv)
    begin(count_copies, has_above, has_below)

    @pl.when(jnp.logical_not(takes_low))
    def _():
        low[...] = jnp.zeros_like(low)

    @pl.when(jnp.logical_not(takes_high))
    def _():
        high[...] = jnp.zeros_like(high)

    turn_load.wait()
    place_load.wait()
    line = lax.broadcasted_iota(jnp.int32, (16, 128), 0)
    odd = (line % 2) == 1
    sign_sin = jnp.where(line % 4 < 2, 1.0, -1.0)
    sign_cos = jnp.where((line % 4 == 0) | (line % 4 == 3), 1.0, -1.0)

    @pl.loop(0, BINS // 16, unroll=2)
    def _(block):
        rows = pl.ds(pl.multiple_of(block * 16, 16), 16)
        shifted = pl.ds(pl.multiple_of(block * 16 + BINS, 16), 16)
        cos = place_table[rows, 0:HALF]
        minus_sin = place_table[rows, HALF : 2 * HALF]
        turn_cos = jnp.broadcast_to(turn_table[rows, 0:1], (16, 128))
        turn_sin = jnp.broadcast_to(turn_table[rows, 1:2], (16, 128))
        for index in range(GROUP):
            table[index, rows, HALF : 2 * HALF] = cos.astype(jnp.bfloat16)
            table[index, shifted, HALF : 2 * HALF] = minus_sin.astype(jnp.bfloat16)
            table[index, rows, 0:HALF] = (jnp.where(odd, minus_sin, cos) * sign_cos).astype(jnp.bfloat16)
            table[index, shifted, 0:HALF] = (jnp.where(odd, cos, minus_sin) * sign_sin).astype(jnp.bfloat16)
            if index < GROUP - 1:
                cos, minus_sin = (
                    cos * turn_cos + minus_sin * turn_sin,
                    minus_sin * turn_cos - cos * turn_sin,
                )

    def level(read, rows):
        square = jnp.zeros((rows, 128), jnp.float32)
        for lane in range(0, 2 * BINS, 128):
            entry = read(slice(lane, lane + 128))
            square = square + entry * entry
        mean = jnp.sum(square, axis=1, keepdims=True) * (1.0 / (2 * BINS))
        return jnp.broadcast_to(inverse_root(mean + 1e-6), (rows, 128))

    own_load.wait()
    mine = count_own[...]
    mask_own = jnp.concatenate([jnp.where(mine > 1.5, 1.0, 0.0)] * 2, axis=0)

    @pl.loop(0, CHANNELS // 16)
    def _(block):
        here = pl.ds(pl.multiple_of(block * 16, 16), 16)
        levels = []
        for window in range(2):
            levels.append(level(lambda lanes: own[window, here, lanes], 16))
            own_level[window, here, :] = levels[window]
        for lane in range(0, BINS, 128):
            real, imag = slice(lane, lane + 128), slice(BINS + lane, BINS + lane + 128)
            powers = []
            for window in range(2):
                re, im = own[window, here, real] * levels[window], own[window, here, imag] * levels[window]
                powers.append(re * re + im * im)
            weight = jnp.broadcast_to(band[:, real], (16, 128))
            own_stack[here, real] = ((powers[0] + mask_own * powers[1]) * weight).astype(jnp.bfloat16)

    def own_piece(step):
        own_term[step] = lax.dot_general(
            own_stack[...],
            table[(member + step) % GROUP, 0:BINS],
            (((1,), (0,)), ((), ())),
            preferred_element_type=jnp.float32,
        )

    @pl.loop(1, GROUP)
    def _(step):
        own_piece(step)
        remote(own_term.at[step], own_got_one.at[step - 1], own_one_send, own_one_recv, in_group(step)).start()

    own_piece(0)

    last_level = own_level.at[:, pl.ds(LAST * ROWS, ROWS)]
    level_copies = both_sides(last_level, level_low, last_level, level_high, level_send, level_recv)
    begin(level_copies, sends_up, sends_down)

    end_recv(count_copies, has_below, has_above)
    end_send(count_copies, has_above, has_below)
    above_count = count_high[...]
    side = jnp.minimum(mine, above_count)
    across = jnp.minimum(count_low[...], above_count)
    row_line = lax.broadcasted_iota(jnp.int32, (8, 128), 0)
    kept[...] = jnp.where(row_line == 0, mine, jnp.where(row_line == 1, side, across))
    for step in range(1, GROUP):
        remote(kept, kept_one.at[step - 1], kept_one_send, kept_one_recv, in_group(step)).start()
    mask_side = jnp.where(side > 1.5, 1.0, 0.0)
    mask_across = jnp.where(across > 1.5, 1.0, 0.0)

    def readers_of(index):
        here = pl.ds(pl.multiple_of(index * ROWS, ROWS), ROWS)

        def reader(kind, window):
            if kind == 0:
                return lambda lanes: own[window, here, lanes]
            ref = low if kind == 1 else high
            return lambda lanes: ref[index, window, :, lanes]

        return {(kind, window): reader(kind, window) for kind in range(3) for window in range(2)}

    def products(readers, levels, begin_lane, end_lane, place=0):
        rows = slice(place * LINES, (place + 1) * LINES)
        for lane in range(begin_lane, end_lane, 128):
            real, imag = slice(lane, lane + 128), slice(BINS + lane, BINS + lane + 128)
            weight = jnp.broadcast_to(band[:, real], (ROWS, 128))
            re = {key: read(real) * levels[key] for key, read in readers.items()}
            im = {key: read(imag) * levels[key] for key, read in readers.items()}

            def cross(a, b, mask):
                parts = []
                for window in range(2):
                    ra, ia, rb, ib = re[a, window], im[a, window], re[b, window], im[b, window]
                    parts.append((ra * rb + ia * ib, ia * rb - ra * ib))
                return (
                    (parts[0][0] + mask * parts[1][0]) * weight,
                    (parts[0][1] + mask * parts[1][1]) * weight,
                )

            side_re, side_im = cross(0, 2, mask_side)
            across_re, across_im = cross(1, 2, mask_across)
            stack[rows, real] = jnp.concatenate([side_re, across_re], axis=0).astype(jnp.bfloat16)
            stack[rows, imag] = jnp.concatenate([side_im, across_im], axis=0).astype(jnp.bfloat16)

    def times_table(lines, step, rows):
        return lax.dot_general(
            stack[0:lines, rows],
            table[(member + step) % GROUP, rows],
            (((1,), (0,)), ((), ())),
            preferred_element_type=jnp.float32,
        )

    def lines_of(unit):
        return LINES if isinstance(unit, int) and unit >= PAIRS else 2 * LINES

    def send_piece(unit, step):
        lines = pl.ds(0, lines_of(unit))
        remote(
            term.at[unit, step, lines], got_one.at[unit, step - 1, lines],
            one_send.at[unit], one_recv.at[unit], in_group(step),
        ).start()

    def cross_spectra(index, place):
        end_recv(halo(index), takes_low, takes_high)
        next_halo(index + AHEAD)
        here = pl.ds(pl.multiple_of(index * ROWS, ROWS), ROWS)
        readers = readers_of(index)
        levels = {
            key: own_level[key[1], here, :] if key[0] == 0 else level(read, ROWS) for key, read in readers.items()
        }
        products(readers, levels, 0, BINS, place)

    def correlate(unit):
        lines = lines_of(unit)

        @pl.loop(1, GROUP)
        def _(step):
            term[unit, step, 0:lines] = times_table(lines, step, slice(0, 2 * BINS))
            send_piece(unit, step)

        term[unit, 0, 0:lines] = times_table(lines, 0, slice(0, 2 * BINS))

    def correlate_last():
        end_recv(level_copies, takes_low, takes_high)
        end_send(level_copies, sends_up, sends_down)
        readers = readers_of(LAST)
        levels = {}
        for window in range(2):
            levels[0, window] = own_level[window, LAST * ROWS : PARTS * ROWS, :]
            levels[1, window] = level_low[window]
            levels[2, window] = level_high[window]
        for run, (start, stop) in enumerate(RUNS):
            for copies in runs(run):
                end_recv(copies, takes_low, takes_high)
            products(readers, levels, start, stop)
            real, imag = slice(start, stop), slice(BINS + start, BINS + stop)

            def piece(step):
                value = times_table(LINES, step, real) + times_table(LINES, step, imag)
                term[UNITS - 1, step, 0:LINES] = value if run == 0 else term[UNITS - 1, step, 0:LINES] + value

            @pl.loop(1, GROUP)
            def _(step):
                piece(step)
                if run == len(RUNS) - 1:
                    send_piece(UNITS - 1, step)

            piece(0)

    def packed(groups, chip):
        lane = lax.broadcasted_iota(jnp.int32, groups[0].shape, 1)
        value = None
        for place in reversed(range(len(groups))):
            shift = ((place - chip) * SHARE) % 128
            moved = pltpu.roll(groups[place], shift, axis=1) if shift else groups[place]
            value = moved if value is None else jnp.where(lane < (place + 1) * SHARE, moved, value)
        return value

    def pieces_of(unit):
        return got_one.at[unit, :, pl.ds(0, lines_of(unit))]

    def add_group(unit):
        whole(pieces_of(unit), one_send.at[unit], one_recv.at[unit]).wait_recv()
        lines = lines_of(unit)
        for half in range(2):
            lanes = slice(half * HALF, (half + 1) * HALF)
            value = term[unit, 0, 0:lines, lanes]
            for step in range(GROUP - 1):
                value = value + got_one[unit, step, 0:lines, lanes]
            groups = [value[start : start + ROWS] for start in range(0, lines, ROWS)]
            for chip in range(RING // 2):
                pack[unit, half * (RING // 2) + chip] = packed(groups, chip)
        for step in range(1, RING):
            remote(
                pack.at[unit, (row + step) % RING], got_two.at[unit, step - 1],
                two_send, two_recv.at[unit], in_ring(step),
            ).start()

    def send_up(index):
        for step in range(RING):
            target = (row + step) % RING
            remote(
                pack.at[index, target], got_two_low.at[index - TAIL, step], two_low_send, two_low_recv.at[index - TAIL],
                (target * GROUP + member, plane + 1),
            ).start()

    def add_group_up(index):
        add_group(index)
        pl.when(has_above)(lambda: send_up(index))

    def sum_ring(index):
        whole(got_two.at[index], two_send, two_recv.at[index]).wait_recv()
        value = pack[index, row]
        for step in range(RING - 1):
            value = value + got_two[index, step]
        total[index] = value

    def add_ring(index):
        sum_ring(index)
        pl.when(has_above)(remote(total.at[index], got_low.at[index], z_send, z_recv, above).start)

    def sum_low(index):
        whole(got_two_low.at[index - TAIL], two_low_send, two_low_recv.at[index - TAIL]).wait_recv()
        value = got_two_low[index - TAIL, 0]
        for step in range(1, RING):
            value = value + got_two_low[index - TAIL, step]
        got_low[index] = value

    def kept_copies():
        return both_sides(kept_all, kept_low, kept_all, kept_high, kept_z_send, kept_z_recv)

    def own_copies():
        return both_sides(own_total, own_low, own_total, own_high, own_z_send, own_z_recv)

    @pl.loop(0, PAIRS)
    def _(unit):
        cross_spectra(2 * unit, 0)
        cross_spectra(2 * unit + 1, 1)
        correlate(unit)

        @pl.when(unit >= 1)
        def _():
            add_group(unit - 1)

        @pl.when(unit >= 2)
        def _():
            add_ring(unit - 2)

        @pl.when(unit == 1)
        def _():
            whole(kept_one, kept_one_send, kept_one_recv).wait()
            value = kept[...]
            for step in range(GROUP - 1):
                value = value + kept_one[step]
            kept_part[...] = value
            whole(own_got_one, own_one_send, own_one_recv).wait()
            for half in range(2):
                lanes = slice(half * HALF, (half + 1) * HALF)
                groups = []
                for block in range(4):
                    rows = slice(block * 16, (block + 1) * 16)
                    value = own_term[0, rows, lanes]
                    for step in range(GROUP - 1):
                        value = value + own_got_one[step, rows, lanes]
                    groups.append(value)
                for chip in range(RING // 2):
                    own_pack[half * (RING // 2) + chip] = packed(groups, chip)
            for step in range(1, RING):
                remote(kept_part, kept_two.at[step - 1], kept_two_send, kept_two_recv, in_ring(step)).start()
                remote(
                    own_pack.at[(row + step) % RING], own_got_two.at[step - 1], own_two_send, own_two_recv, in_ring(step)
                ).start()

        @pl.when(unit == 2)
        def _():
            whole(kept_two, kept_two_send, kept_two_recv).wait()
            whole(own_got_two, own_two_send, own_two_recv).wait()
            value = kept_part[...]
            own_value = own_pack[row]
            for step in range(RING - 1):
                value = value + kept_two[step]
                own_value = own_value + own_got_two[step]
            kept_all[...] = value
            own_total[...] = own_value
            begin(kept_copies(), has_above, has_below)
            begin(own_copies(), has_above, has_below)

    cross_spectra(LAST - 1, 0)
    correlate(PAIRS)
    correlate_last()
    add_ring(TAIL - 1)
    add_group_up(TAIL)
    add_group_up(PAIRS)
    pairs_load.wait()
    live_load.wait()
    for copies in (kept_copies(), own_copies()):
        end_recv(copies, has_below, has_above)
        end_send(copies, has_above, has_below)
    for place, source in enumerate((own_low, own_total, own_high)):
        value = source[...]
        for block in range(4):
            rows = slice(block * 16, (block + 1) * 16)
            own_wide[place, rows, :] = pltpu.roll(value, 128 - block * SHARE, axis=1) if block else value
    add_group_up(UNITS - 1)

    kept_options = [
        kept_low[0:1], kept_low[1:2], kept_all[2:3], kept_all[0:1], kept_all[1:2], kept_high[0:1],
    ]

    def choose(slot, options):
        a, b = pairs[0, 0, slot], pairs[0, 1, slot]
        tests = [
            (a == plane - 1) & (b == plane),
            (a == plane - 1) & (b == plane + 1),
            (a == plane) & (b == plane),
            (a == plane) & (b == plane + 1),
            (a == plane + 1) & (b == plane + 1),
        ]
        value = options[0]
        for test, option in zip(tests, options[1:]):
            value = jnp.where(test, option, value)
        return value

    scales = []
    for slot in range(SLOTS):
        alive = (slot < live[0]).astype(jnp.float32)
        scales.append(jnp.broadcast_to(alive / choose(slot, kept_options), (ROWS, 128)))

    def fill(unit):
        for part in range(2 if unit < PAIRS else 1):
            index = 2 * unit + part if unit < PAIRS else LAST - UNITS + 1 + unit
            rows = slice(index * ROWS, (index + 1) * ROWS)
            lane = part * 2 * SHARE

            def side(tile):
                return pltpu.roll(tile, 128 - lane, axis=1) if lane else tile

            options = [
                own_wide[0, rows], side(got_low[unit]), pltpu.roll(total[unit], 128 - SHARE - lane, axis=1),
                own_wide[1, rows], side(total[unit]), own_wide[2, rows],
            ]
            for slot in range(SLOTS):
                start = slot * CHANNELS + index * ROWS
                chosen[start : start + ROWS, :] = choose(slot, options) * scales[slot]

    def settle(unit):
        sum_ring(unit)
        pl.when(has_below)(lambda: sum_low(unit))
        fill(unit)

    early = got_low.at[pl.ds(0, TAIL)]
    pl.when(has_below)(whole(early, z_send, z_recv).wait_recv)
    for unit in range(TAIL):
        fill(unit)
    pl.when(has_above)(whole(early, z_send, z_recv).wait_send)
    for unit in range(TAIL, UNITS - 1):
        settle(unit)
    for unit in range(UNITS):
        whole(pieces_of(unit), one_send.at[unit], one_recv.at[unit]).wait_send()
    for index in range(LAST):
        end_send(halo(index), sends_up, sends_down)
    for run in range(len(RUNS)):
        for copies in runs(run):
            end_send(copies, sends_up, sends_down)
    settle(UNITS - 1)
    for block in range(SLOTS * CHANNELS // 128):
        lanes = slice(block * 128, (block + 1) * 128)
        out[:, lanes] = chosen[lanes, :].T[:SHARE]
    whole(got_two, two_send, two_recv.at[0]).wait_send()
    pl.when(has_above)(whole(got_two_low, two_low_send, two_low_recv.at[0]).wait_send)


def on_device(spectra, counts, band_filter, pair_list, live_slots):
    turns, places = twiddles()
    f32, bf16, i32 = jnp.float32, jnp.bfloat16, jnp.int32
    dma = pltpu.SemaphoreType.DMA
    tile = (8, 128)
    vmem = pltpu.VMEM
    anywhere = pl.BlockSpec(memory_space=pl.ANY)
    far = pl.BlockSpec(memory_space=pltpu.HBM)
    return pl.pallas_call(
        kernel,
        out_shape=jax.ShapeDtypeStruct((SHARE, SLOTS * CHANNELS), f32),
        in_specs=[anywhere, far, pl.BlockSpec(memory_space=vmem), far, far, anywhere, anywhere],
        out_specs=pl.BlockSpec(memory_space=vmem),
        scratch_shapes=[
            pltpu.SMEM((1, 1), i32), pltpu.SMEM((1, 2, SLOTS), i32), pltpu.SMEM((1,), i32),
            vmem((2, CHANNELS, 2 * BINS), f32),
            vmem((2, CHANNELS, 128), f32),
            vmem((PARTS, 2, ROWS, 2 * BINS), f32),
            vmem((PARTS, 2, ROWS, 2 * BINS), f32),
            vmem((BINS, 128), f32),
            vmem((BINS, 2 * HALF), f32),
            vmem((GROUP, 2 * BINS, PIECE), bf16),
            vmem((CHANNELS, BINS), bf16),
            vmem((GROUP, CHANNELS, PIECE), f32),
            vmem((GROUP - 1, CHANNELS, PIECE), f32),
            vmem((RING, 16, 128), f32),
            vmem((RING - 1, 16, 128), f32),
            vmem((16, 128), f32), vmem((16, 128), f32), vmem((16, 128), f32),
            vmem((3, CHANNELS, 128), f32),
            vmem((2 * LINES, 2 * BINS), bf16),
            vmem((UNITS, GROUP, 2 * LINES, PIECE), f32),
            vmem((UNITS, GROUP - 1, 2 * LINES, PIECE), f32),
            vmem((UNITS, RING) + tile, f32),
            vmem((UNITS, RING - 1) + tile, f32),
            vmem((UNITS - TAIL, RING) + tile, f32),
            vmem((UNITS,) + tile, f32),
            vmem((UNITS,) + tile, f32),
            vmem((SLOTS * CHANNELS, 128), f32),
            vmem((2,) + tile, f32), vmem((2,) + tile, f32),
            vmem(tile, f32), vmem(tile, f32), vmem(tile, f32),
            vmem(tile, f32),
            vmem((GROUP - 1,) + tile, f32),
            vmem(tile, f32),
            vmem((RING - 1,) + tile, f32),
            vmem(tile, f32), vmem(tile, f32), vmem(tile, f32),
            dma((6,)),
            dma((PARTS, 2)), dma((PARTS, 2)),
            dma((UNITS,)), dma((UNITS,)),
            dma, dma((UNITS,)),
            dma, dma((UNITS - TAIL,)),
            dma, dma,
            dma((len(RUNS), 2, 2)), dma((len(RUNS), 2, 2)),
            dma((2,)), dma((2,)),
            dma, dma, dma, dma,
            dma((2,)), dma((2,)),
            dma((2,)), dma((2,)),
            dma, dma, dma, dma,
            dma((2,)), dma((2,)),
        ],
        compiler_params=pltpu.CompilerParams(
            collective_id=0, has_side_effects=True, vmem_limit_bytes=56 * 1024 * 1024
        ),
    )(
        spectra, counts, band_filter.reshape(1, BINS), jnp.swapaxes(pair_list, 1, 2), live_slots,
        jnp.asarray(turns), jnp.asarray(places),
    )


def solution(mesh):
    placed = (P("win", "pair", None, None), P("win", "pair"), P(), P("pair", None, None), P("pair"))
    return jax.shard_map(
        on_device, mesh=mesh, in_specs=placed, out_specs=P("win", "pair"), check_vma=False
    )
```

```python
import math

import jax
import jax.numpy as jnp
import numpy as np
from jax import lax
from jax.experimental import pallas as pl
from jax.experimental.pallas import tpu as pltpu
from jax.sharding import PartitionSpec as P

LAGS = 2048
BINS = 2048
CHANNELS = 64
SLOTS = 6
ROWS = 8
PARTS = CHANNELS // ROWS
GROUP = 8
RING = 8
SHARE = LAGS // (GROUP * RING)
PIECE = SHARE * RING
HALF = PIECE // 2
LINES = 2 * ROWS
AHEAD = 2
LAST = PARTS - 1
RUNS = ((0, 1280), (1280, BINS))
PAIRS = 3
UNITS = PAIRS + 2
TAIL = PAIRS - 1
FAR_FIRST = (4, 3, 5, 2, 6, 1, 7)
MESH = pl.DeviceIdType.MESH


def far_first(count):
    return GROUP // 2 + (count // 2) * ((count % 2) * 2 - 1)


def twiddles():
    frequency = np.arange(BINS, dtype=np.int64)[:, None]
    lane = np.arange(HALF, dtype=np.int64)
    place = (lane // SHARE) * PIECE + lane % SHARE

    def wave(offsets):
        angle = np.mod(frequency * offsets[None, :], 2 * BINS) * (math.pi / BINS)
        return np.cos(angle), np.sin(angle)

    turns = np.zeros((BINS, 128), np.float32)
    turn_cos, turn_sin = wave(np.array([SHARE], np.int64))
    turns[:, 0:1], turns[:, 1:2] = turn_cos, turn_sin
    place_cos, place_sin = wave(place)
    places = np.concatenate([place_cos, -place_sin], axis=1) * math.sqrt(2.0 / BINS)
    return turns, places.astype(np.float32)


def inverse_root(value):
    root = lax.rsqrt(value)
    return root * (1.5 - 0.5 * value * root * root)


def kernel(
    spectra, counts_hbm, band, pairs_hbm, live_hbm, turns, places, out,
    counts, pairs, live,
    own, own_level, low, high, turn_table, place_table, table,
    own_stack, own_term, own_got_one, own_pack, own_got_two, own_total, own_low, own_high, own_wide,
    stack, term, got_one, pack, got_two, got_two_low, total, got_low, chosen, level_low, level_high,
    count_own, count_low, count_high, kept, kept_one, kept_part, kept_two, kept_all, kept_low, kept_high,
    load_sem, halo_send, halo_recv, one_send, one_recv, two_send, two_recv, two_low_send, two_low_recv, z_send, z_recv,
    run_send, run_recv, level_send, level_recv,
    own_one_send, own_one_recv, own_two_send, own_two_recv, own_z_send, own_z_recv,
    count_send, count_recv, kept_one_send, kept_one_recv, kept_two_send, kept_two_recv, kept_z_send, kept_z_recv,
):
    win = lax.axis_index("win")
    plane = lax.axis_index("pair")
    row = win // GROUP
    member = win % GROUP
    above = (win, (plane + 1) % RING)
    below = (win, (plane + RING - 1) % RING)
    has_above, has_below = plane < RING - 1, plane > 0
    sends_up, takes_low = plane < RING - 2, (plane > 0) & (plane < RING - 1)
    sends_down, takes_high = plane > 0, plane < RING - 1

    def in_group(step):
        return (row * GROUP + (member + step) % GROUP, plane)

    def in_ring(step):
        return (((row + step) % RING) * GROUP + member, plane)

    for ref in (count_low, count_high, kept_low, kept_high):
        ref[...] = jnp.ones_like(ref)
    for ref in (own_low, own_high, got_low, level_low, level_high):
        ref[...] = jnp.zeros_like(ref)

    barrier = pltpu.get_barrier_semaphore()

    @pl.when(has_above)
    def _():
        pl.semaphore_signal(barrier, inc=1, device_id=above, device_id_type=MESH)

    @pl.when(has_below)
    def _():
        pl.semaphore_signal(barrier, inc=1, device_id=below, device_id_type=MESH)

    for step in range(1, GROUP):
        pl.semaphore_signal(barrier, inc=1, device_id=in_group(step), device_id_type=MESH)
    for step in range(1, RING):
        pl.semaphore_signal(barrier, inc=1, device_id=in_ring(step), device_id_type=MESH)

    count_load = pltpu.make_async_copy(counts_hbm, counts, load_sem.at[0])
    pairs_load = pltpu.make_async_copy(pairs_hbm, pairs, load_sem.at[1])
    live_load = pltpu.make_async_copy(live_hbm, live, load_sem.at[2])
    turn_load = pltpu.make_async_copy(turns, turn_table, load_sem.at[3])
    place_load = pltpu.make_async_copy(places, place_table, load_sem.at[4])
    own_load = pltpu.make_async_copy(spectra.at[:, 0], own, load_sem.at[5])
    for load in (count_load, pairs_load, live_load, turn_load, place_load, own_load):
        load.start()
    count_load.wait()
    count_own[...] = jnp.full((8, 128), counts[0, 0].astype(jnp.float32))
    pl.semaphore_wait(barrier, GROUP - 1 + RING - 1 + has_above.astype(jnp.int32) + has_below.astype(jnp.int32))

    def remote(source, target, send, recv, device):
        return pltpu.make_async_remote_copy(
            src_ref=source, dst_ref=target, send_sem=send, recv_sem=recv, device_id=device, device_id_type=MESH
        )

    def whole(ref, send, recv):
        return remote(ref, ref, send, recv, above)

    def both_sides(up, low_ref, down, high_ref, send, recv):
        return (
            remote(up, low_ref, send.at[0], recv.at[0], above),
            remote(down, high_ref, send.at[1], recv.at[1], below),
        )

    def halo(index):
        block = spectra.at[:, 0, pl.ds(pl.multiple_of(index * ROWS, ROWS), ROWS), :]
        return both_sides(block, low.at[index], block, high.at[index], halo_send.at[index], halo_recv.at[index])

    def runs(run):
        copies = []
        for side in range(2):
            lanes = pl.ds(side * BINS + RUNS[run][0], RUNS[run][1] - RUNS[run][0])
            block = spectra.at[:, 0, pl.ds(LAST * ROWS, ROWS), lanes]
            copies.append(
                both_sides(
                    block, low.at[LAST, :, :, lanes], block, high.at[LAST, :, :, lanes],
                    run_send.at[run, side], run_recv.at[run, side],
                )
            )
        return copies

    def next_halo(index):
        within = index < LAST
        begin(halo(lax.rem(index, PARTS)), sends_up & within, sends_down & within)
        for run in range(len(RUNS)):
            for copies in runs(run):
                begin(copies, sends_up & (index == LAST + run), sends_down & (index == LAST + run))

    def begin(copies, up, down):
        pl.when(up)(copies[0].start)
        pl.when(down)(copies[1].start)

    def end_send(copies, up, down):
        pl.when(up)(copies[0].wait_send)
        pl.when(down)(copies[1].wait_send)

    def end_recv(copies, takes_low, takes_high):
        pl.when(takes_low)(copies[0].wait_recv)
        pl.when(takes_high)(copies[1].wait_recv)

    for index in range(AHEAD):
        begin(halo(index), sends_up, sends_down)
    count_copies = both_sides(count_own, count_low, count_own, count_high, count_send, count_recv)
    begin(count_copies, has_above, has_below)

    @pl.when(jnp.logical_not(takes_low))
    def _():
        low[...] = jnp.zeros_like(low)

    @pl.when(jnp.logical_not(takes_high))
    def _():
        high[...] = jnp.zeros_like(high)

    turn_load.wait()
    place_load.wait()
    line = lax.broadcasted_iota(jnp.int32, (16, 128), 0)
    odd = (line % 2) == 1
    sign_sin = jnp.where(line % 4 < 2, 1.0, -1.0)
    sign_cos = jnp.where((line % 4 == 0) | (line % 4 == 3), 1.0, -1.0)

    @pl.loop(0, BINS // 16, unroll=2)
    def _(block):
        rows = pl.ds(pl.multiple_of(block * 16, 16), 16)
        shifted = pl.ds(pl.multiple_of(block * 16 + BINS, 16), 16)
        cos = place_table[rows, 0:HALF]
        minus_sin = place_table[rows, HALF : 2 * HALF]
        turn_cos = jnp.broadcast_to(turn_table[rows, 0:1], (16, 128))
        turn_sin = jnp.broadcast_to(turn_table[rows, 1:2], (16, 128))
        for index in range(GROUP):
            table[index, rows, HALF : 2 * HALF] = cos.astype(jnp.bfloat16)
            table[index, shifted, HALF : 2 * HALF] = minus_sin.astype(jnp.bfloat16)
            table[index, rows, 0:HALF] = (jnp.where(odd, minus_sin, cos) * sign_cos).astype(jnp.bfloat16)
            table[index, shifted, 0:HALF] = (jnp.where(odd, cos, minus_sin) * sign_sin).astype(jnp.bfloat16)
            if index < GROUP - 1:
                cos, minus_sin = (
                    cos * turn_cos + minus_sin * turn_sin,
                    minus_sin * turn_cos - cos * turn_sin,
                )

    def level(read, rows):
        square = jnp.zeros((rows, 128), jnp.float32)
        for lane in range(0, 2 * BINS, 128):
            entry = read(slice(lane, lane + 128))
            square = square + entry * entry
        mean = jnp.sum(square, axis=1, keepdims=True) * (1.0 / (2 * BINS))
        return jnp.broadcast_to(inverse_root(mean + 1e-6), (rows, 128))

    own_load.wait()
    mine = count_own[...]
    mask_own = jnp.concatenate([jnp.where(mine > 1.5, 1.0, 0.0)] * 2, axis=0)

    @pl.loop(0, CHANNELS // 16)
    def _(block):
        here = pl.ds(pl.multiple_of(block * 16, 16), 16)
        levels = []
        for window in range(2):
            levels.append(level(lambda lanes: own[window, here, lanes], 16))
            own_level[window, here, :] = levels[window]
        for lane in range(0, BINS, 128):
            real, imag = slice(lane, lane + 128), slice(BINS + lane, BINS + lane + 128)
            powers = []
            for window in range(2):
                re, im = own[window, here, real] * levels[window], own[window, here, imag] * levels[window]
                powers.append(re * re + im * im)
            weight = jnp.broadcast_to(band[:, real], (16, 128))
            own_stack[here, real] = ((powers[0] + mask_own * powers[1]) * weight).astype(jnp.bfloat16)

    def own_piece(step):
        own_term[step] = lax.dot_general(
            own_stack[...],
            table[(member + step) % GROUP, 0:BINS],
            (((1,), (0,)), ((), ())),
            preferred_element_type=jnp.float32,
        )

    @pl.loop(1, GROUP)
    def _(step):
        own_piece(step)
        remote(own_term.at[step], own_got_one.at[step - 1], own_one_send, own_one_recv, in_group(step)).start()

    own_piece(0)

    last_level = own_level.at[:, pl.ds(LAST * ROWS, ROWS)]
    level_copies = both_sides(last_level, level_low, last_level, level_high, level_send, level_recv)
    begin(level_copies, sends_up, sends_down)

    end_recv(count_copies, has_below, has_above)
    end_send(count_copies, has_above, has_below)
    above_count = count_high[...]
    side = jnp.minimum(mine, above_count)
    across = jnp.minimum(count_low[...], above_count)
    row_line = lax.broadcasted_iota(jnp.int32, (8, 128), 0)
    kept[...] = jnp.where(row_line == 0, mine, jnp.where(row_line == 1, side, across))
    for step in range(1, GROUP):
        remote(kept, kept_one.at[step - 1], kept_one_send, kept_one_recv, in_group(step)).start()
    mask_side = jnp.where(side > 1.5, 1.0, 0.0)
    mask_across = jnp.where(across > 1.5, 1.0, 0.0)

    def readers_of(index):
        here = pl.ds(pl.multiple_of(index * ROWS, ROWS), ROWS)

        def reader(kind, window):
            if kind == 0:
                return lambda lanes: own[window, here, lanes]
            ref = low if kind == 1 else high
            return lambda lanes: ref[index, window, :, lanes]

        return {(kind, window): reader(kind, window) for kind in range(3) for window in range(2)}

    def products(readers, levels, begin_lane, end_lane, place=0):
        rows = slice(place * LINES, (place + 1) * LINES)
        for lane in range(begin_lane, end_lane, 128):
            real, imag = slice(lane, lane + 128), slice(BINS + lane, BINS + lane + 128)
            weight = jnp.broadcast_to(band[:, real], (ROWS, 128))
            re = {key: read(real) * levels[key] for key, read in readers.items()}
            im = {key: read(imag) * levels[key] for key, read in readers.items()}

            def cross(a, b, mask):
                parts = []
                for window in range(2):
                    ra, ia, rb, ib = re[a, window], im[a, window], re[b, window], im[b, window]
                    parts.append((ra * rb + ia * ib, ia * rb - ra * ib))
                return (
                    (parts[0][0] + mask * parts[1][0]) * weight,
                    (parts[0][1] + mask * parts[1][1]) * weight,
                )

            side_re, side_im = cross(0, 2, mask_side)
            across_re, across_im = cross(1, 2, mask_across)
            stack[rows, real] = jnp.concatenate([side_re, across_re], axis=0).astype(jnp.bfloat16)
            stack[rows, imag] = jnp.concatenate([side_im, across_im], axis=0).astype(jnp.bfloat16)

    def times_table(lines, step, rows):
        return lax.dot_general(
            stack[0:lines, rows],
            table[(member + step) % GROUP, rows],
            (((1,), (0,)), ((), ())),
            preferred_element_type=jnp.float32,
        )

    def lines_of(unit):
        return LINES if isinstance(unit, int) and unit >= PAIRS else 2 * LINES

    def send_piece(unit, step):
        lines = pl.ds(0, lines_of(unit))
        remote(
            term.at[unit, step, lines], got_one.at[unit, step - 1, lines],
            one_send.at[unit], one_recv.at[unit], in_group(step),
        ).start()

    def cross_spectra(index, place):
        end_recv(halo(index), takes_low, takes_high)
        next_halo(index + AHEAD)
        here = pl.ds(pl.multiple_of(index * ROWS, ROWS), ROWS)
        readers = readers_of(index)
        levels = {
            key: own_level[key[1], here, :] if key[0] == 0 else level(read, ROWS) for key, read in readers.items()
        }
        products(readers, levels, 0, BINS, place)

    def correlate(unit):
        lines = lines_of(unit)

        @pl.loop(1, GROUP)
        def _(count):
            step = far_first(count)
            term[unit, step, 0:lines] = times_table(lines, step, slice(0, 2 * BINS))
            send_piece(unit, step)

        term[unit, 0, 0:lines] = times_table(lines, 0, slice(0, 2 * BINS))

    def correlate_last():
        end_recv(level_copies, takes_low, takes_high)
        end_send(level_copies, sends_up, sends_down)
        readers = readers_of(LAST)
        levels = {}
        for window in range(2):
            levels[0, window] = own_level[window, LAST * ROWS : PARTS * ROWS, :]
            levels[1, window] = level_low[window]
            levels[2, window] = level_high[window]
        for run, (start, stop) in enumerate(RUNS):
            for copies in runs(run):
                end_recv(copies, takes_low, takes_high)
            products(readers, levels, start, stop)
            real, imag = slice(start, stop), slice(BINS + start, BINS + stop)

            def piece(step):
                value = times_table(LINES, step, real) + times_table(LINES, step, imag)
                term[UNITS - 1, step, 0:LINES] = value if run == 0 else term[UNITS - 1, step, 0:LINES] + value

            @pl.loop(1, GROUP)
            def _(count):
                step = far_first(count)
                piece(step)
                if run == len(RUNS) - 1:
                    send_piece(UNITS - 1, step)

            piece(0)

    def packed(groups, chip):
        lane = lax.broadcasted_iota(jnp.int32, groups[0].shape, 1)
        value = None
        for place in reversed(range(len(groups))):
            shift = ((place - chip) * SHARE) % 128
            moved = pltpu.roll(groups[place], shift, axis=1) if shift else groups[place]
            value = moved if value is None else jnp.where(lane < (place + 1) * SHARE, moved, value)
        return value

    def pieces_of(unit):
        return got_one.at[unit, :, pl.ds(0, lines_of(unit))]

    def add_group(unit, up=False):
        whole(pieces_of(unit), one_send.at[unit], one_recv.at[unit]).wait_recv()
        lines = lines_of(unit)
        for half in range(2):
            lanes = slice(half * HALF, (half + 1) * HALF)
            value = term[unit, 0, 0:lines, lanes]
            for step in range(GROUP - 1):
                value = value + got_one[unit, step, 0:lines, lanes]
            groups = [value[start : start + ROWS] for start in range(0, lines, ROWS)]
            for chip in range(RING // 2):
                pack[unit, half * (RING // 2) + chip] = packed(groups, chip)
        for step in FAR_FIRST:
            if up:
                pl.when(has_above)(piece_up(unit, step).start)
            remote(
                pack.at[unit, (row + step) % RING], got_two.at[unit, step - 1],
                two_send, two_recv.at[unit], in_ring(step),
            ).start()
        if up:
            pl.when(has_above)(piece_up(unit, 0).start)

    def piece_up(unit, step):
        target = (row + step) % RING
        return remote(
            pack.at[unit, target], got_two_low.at[unit - TAIL, step], two_low_send, two_low_recv.at[unit - TAIL],
            (target * GROUP + member, plane + 1),
        )

    def sum_ring(index):
        whole(got_two.at[index], two_send, two_recv.at[index]).wait_recv()
        value = pack[index, row]
        for step in range(RING - 1):
            value = value + got_two[index, step]
        total[index] = value

    def add_ring(index):
        sum_ring(index)
        pl.when(has_above)(remote(total.at[index], got_low.at[index], z_send, z_recv, above).start)

    def sum_low(index):
        whole(got_two_low.at[index - TAIL], two_low_send, two_low_recv.at[index - TAIL]).wait_recv()
        value = got_two_low[index - TAIL, 0]
        for step in range(1, RING):
            value = value + got_two_low[index - TAIL, step]
        got_low[index] = value

    def kept_copies():
        return both_sides(kept_all, kept_low, kept_all, kept_high, kept_z_send, kept_z_recv)

    def own_copies():
        return both_sides(own_total, own_low, own_total, own_high, own_z_send, own_z_recv)

    @pl.loop(0, PAIRS)
    def _(unit):
        cross_spectra(2 * unit, 0)
        cross_spectra(2 * unit + 1, 1)
        correlate(unit)

        @pl.when(unit >= 1)
        def _():
            add_group(unit - 1)

        @pl.when(unit >= 2)
        def _():
            add_ring(unit - 2)

        @pl.when(unit == 1)
        def _():
            whole(kept_one, kept_one_send, kept_one_recv).wait()
            value = kept[...]
            for step in range(GROUP - 1):
                value = value + kept_one[step]
            kept_part[...] = value
            whole(own_got_one, own_one_send, own_one_recv).wait()
            for half in range(2):
                lanes = slice(half * HALF, (half + 1) * HALF)
                groups = []
                for block in range(4):
                    rows = slice(block * 16, (block + 1) * 16)
                    value = own_term[0, rows, lanes]
                    for step in range(GROUP - 1):
                        value = value + own_got_one[step, rows, lanes]
                    groups.append(value)
                for chip in range(RING // 2):
                    own_pack[half * (RING // 2) + chip] = packed(groups, chip)
            for step in range(1, RING):
                remote(kept_part, kept_two.at[step - 1], kept_two_send, kept_two_recv, in_ring(step)).start()
                remote(
                    own_pack.at[(row + step) % RING], own_got_two.at[step - 1], own_two_send, own_two_recv, in_ring(step)
                ).start()

        @pl.when(unit == 2)
        def _():
            whole(kept_two, kept_two_send, kept_two_recv).wait()
            whole(own_got_two, own_two_send, own_two_recv).wait()
            value = kept_part[...]
            own_value = own_pack[row]
            for step in range(RING - 1):
                value = value + kept_two[step]
                own_value = own_value + own_got_two[step]
            kept_all[...] = value
            own_total[...] = own_value
            begin(kept_copies(), has_above, has_below)
            begin(own_copies(), has_above, has_below)

    cross_spectra(LAST - 1, 0)
    correlate(PAIRS)
    correlate_last()
    add_ring(TAIL - 1)
    add_group(TAIL, up=True)
    add_group(PAIRS, up=True)
    pairs_load.wait()
    live_load.wait()
    for copies in (kept_copies(), own_copies()):
        end_recv(copies, has_below, has_above)
        end_send(copies, has_above, has_below)
    for place, source in enumerate((own_low, own_total, own_high)):
        value = source[...]
        for block in range(4):
            rows = slice(block * 16, (block + 1) * 16)
            own_wide[place, rows, :] = pltpu.roll(value, 128 - block * SHARE, axis=1) if block else value
    add_group(UNITS - 1, up=True)

    kept_options = [
        kept_low[0:1], kept_low[1:2], kept_all[2:3], kept_all[0:1], kept_all[1:2], kept_high[0:1],
    ]

    def choose(slot, options):
        a, b = pairs[0, 0, slot], pairs[0, 1, slot]
        tests = [
            (a == plane - 1) & (b == plane),
            (a == plane - 1) & (b == plane + 1),
            (a == plane) & (b == plane),
            (a == plane) & (b == plane + 1),
            (a == plane + 1) & (b == plane + 1),
        ]
        value = options[0]
        for test, option in zip(tests, options[1:]):
            value = jnp.where(test, option, value)
        return value

    scales = []
    for slot in range(SLOTS):
        alive = (slot < live[0]).astype(jnp.float32)
        scales.append(jnp.broadcast_to(alive / choose(slot, kept_options), (ROWS, 128)))

    def fill(unit):
        for part in range(2 if unit < PAIRS else 1):
            index = 2 * unit + part if unit < PAIRS else LAST - UNITS + 1 + unit
            rows = slice(index * ROWS, (index + 1) * ROWS)
            lane = part * 2 * SHARE

            def side(tile):
                return pltpu.roll(tile, 128 - lane, axis=1) if lane else tile

            options = [
                own_wide[0, rows], side(got_low[unit]), pltpu.roll(total[unit], 128 - SHARE - lane, axis=1),
                own_wide[1, rows], side(total[unit]), own_wide[2, rows],
            ]
            for slot in range(SLOTS):
                start = slot * CHANNELS + index * ROWS
                chosen[start : start + ROWS, :] = choose(slot, options) * scales[slot]

    def settle(unit):
        sum_ring(unit)
        pl.when(has_below)(lambda: sum_low(unit))
        fill(unit)

    early = got_low.at[pl.ds(0, TAIL)]
    pl.when(has_below)(whole(early, z_send, z_recv).wait_recv)
    for unit in range(TAIL):
        fill(unit)
    pl.when(has_above)(whole(early, z_send, z_recv).wait_send)
    for unit in range(TAIL, UNITS - 1):
        settle(unit)
    for unit in range(UNITS):
        whole(pieces_of(unit), one_send.at[unit], one_recv.at[unit]).wait_send()
    for index in range(LAST):
        end_send(halo(index), sends_up, sends_down)
    for run in range(len(RUNS)):
        for copies in runs(run):
            end_send(copies, sends_up, sends_down)
    settle(UNITS - 1)
    for block in range(SLOTS * CHANNELS // 128):
        lanes = slice(block * 128, (block + 1) * 128)
        out[:, lanes] = chosen[lanes, :].T[:SHARE]
    whole(got_two, two_send, two_recv.at[0]).wait_send()
    pl.when(has_above)(whole(got_two_low, two_low_send, two_low_recv.at[0]).wait_send)


def on_device(spectra, counts, band_filter, pair_list, live_slots):
    turns, places = twiddles()
    f32, bf16, i32 = jnp.float32, jnp.bfloat16, jnp.int32
    dma = pltpu.SemaphoreType.DMA
    tile = (8, 128)
    vmem = pltpu.VMEM
    anywhere = pl.BlockSpec(memory_space=pl.ANY)
    far = pl.BlockSpec(memory_space=pltpu.HBM)
    return pl.pallas_call(
        kernel,
        out_shape=jax.ShapeDtypeStruct((SHARE, SLOTS * CHANNELS), f32),
        in_specs=[anywhere, far, pl.BlockSpec(memory_space=vmem), far, far, anywhere, anywhere],
        out_specs=pl.BlockSpec(memory_space=vmem),
        scratch_shapes=[
            pltpu.SMEM((1, 1), i32), pltpu.SMEM((1, 2, SLOTS), i32), pltpu.SMEM((1,), i32),
            vmem((2, CHANNELS, 2 * BINS), f32),
            vmem((2, CHANNELS, 128), f32),
            vmem((PARTS, 2, ROWS, 2 * BINS), f32),
            vmem((PARTS, 2, ROWS, 2 * BINS), f32),
            vmem((BINS, 128), f32),
            vmem((BINS, 2 * HALF), f32),
            vmem((GROUP, 2 * BINS, PIECE), bf16),
            vmem((CHANNELS, BINS), bf16),
            vmem((GROUP, CHANNELS, PIECE), f32),
            vmem((GROUP - 1, CHANNELS, PIECE), f32),
            vmem((RING, 16, 128), f32),
            vmem((RING - 1, 16, 128), f32),
            vmem((16, 128), f32), vmem((16, 128), f32), vmem((16, 128), f32),
            vmem((3, CHANNELS, 128), f32),
            vmem((2 * LINES, 2 * BINS), bf16),
            vmem((UNITS, GROUP, 2 * LINES, PIECE), f32),
            vmem((UNITS, GROUP - 1, 2 * LINES, PIECE), f32),
            vmem((UNITS, RING) + tile, f32),
            vmem((UNITS, RING - 1) + tile, f32),
            vmem((UNITS - TAIL, RING) + tile, f32),
            vmem((UNITS,) + tile, f32),
            vmem((UNITS,) + tile, f32),
            vmem((SLOTS * CHANNELS, 128), f32),
            vmem((2,) + tile, f32), vmem((2,) + tile, f32),
            vmem(tile, f32), vmem(tile, f32), vmem(tile, f32),
            vmem(tile, f32),
            vmem((GROUP - 1,) + tile, f32),
            vmem(tile, f32),
            vmem((RING - 1,) + tile, f32),
            vmem(tile, f32), vmem(tile, f32), vmem(tile, f32),
            dma((6,)),
            dma((PARTS, 2)), dma((PARTS, 2)),
            dma((UNITS,)), dma((UNITS,)),
            dma, dma((UNITS,)),
            dma, dma((UNITS - TAIL,)),
            dma, dma,
            dma((len(RUNS), 2, 2)), dma((len(RUNS), 2, 2)),
            dma((2,)), dma((2,)),
            dma, dma, dma, dma,
            dma((2,)), dma((2,)),
            dma((2,)), dma((2,)),
            dma, dma, dma, dma,
            dma((2,)), dma((2,)),
        ],
        compiler_params=pltpu.CompilerParams(
            collective_id=0, has_side_effects=True, vmem_limit_bytes=56 * 1024 * 1024
        ),
    )(
        spectra, counts, band_filter.reshape(1, BINS), jnp.swapaxes(pair_list, 1, 2), live_slots,
        jnp.asarray(turns), jnp.asarray(places),
    )


def solution(mesh):
    placed = (P("win", "pair", None, None), P("win", "pair"), P(), P("pair", None, None), P("pair"))
    return jax.shard_map(
        on_device, mesh=mesh, in_specs=placed, out_specs=P("win", "pair"), check_vma=False
    )
```

```python
import math

import jax
import jax.numpy as jnp
import numpy as np
from jax import lax
from jax.experimental import pallas as pl
from jax.experimental.pallas import tpu as pltpu
from jax.sharding import PartitionSpec as P

LAGS = 2048
BINS = 2048
CHANNELS = 64
SLOTS = 6
ROWS = 8
PARTS = CHANNELS // ROWS
GROUP = 8
RING = 8
SHARE = LAGS // (GROUP * RING)
PIECE = SHARE * RING
HALF = PIECE // 2
LINES = 2 * ROWS
AHEAD = 2
LAST = PARTS - 1
RUNS = ((0, 1280), (1280, BINS))
PAIRS = 3
UNITS = PAIRS + 2
TAIL = PAIRS - 1
FAR_FIRST = (4, 3, 5, 2, 6, 1, 7)
MESH = pl.DeviceIdType.MESH


def far_first(count):
    return GROUP // 2 + (count // 2) * ((count % 2) * 2 - 1)


def twiddles():
    frequency = np.arange(BINS, dtype=np.int64)[:, None]
    lane = np.arange(HALF, dtype=np.int64)
    place = (lane // SHARE) * PIECE + lane % SHARE

    def wave(offsets):
        angle = np.mod(frequency * offsets[None, :], 2 * BINS) * (math.pi / BINS)
        return np.cos(angle), np.sin(angle)

    turns = np.zeros((BINS, 128), np.float32)
    turn_cos, turn_sin = wave(np.array([SHARE], np.int64))
    turns[:, 0:1], turns[:, 1:2] = turn_cos, turn_sin
    place_cos, place_sin = wave(place)
    places = np.concatenate([place_cos, -place_sin], axis=1) * math.sqrt(2.0 / BINS)
    return turns, places.astype(np.float32)


def inverse_root(value):
    root = lax.rsqrt(value)
    return root * (1.5 - 0.5 * value * root * root)


def kernel(
    spectra, counts_hbm, band, pairs_hbm, live_hbm, turns, places, out,
    counts, pairs, live,
    own, own_level, low, high, turn_table, place_table, table,
    own_stack, own_term, own_got_one, own_pack, own_got_two, own_total, own_low, own_high, own_wide,
    stack, term, got_one, pack, got_two, got_two_low, total, got_low, chosen, level_low, level_high,
    count_own, count_low, count_high, kept, kept_one, kept_part, kept_two, kept_all, kept_low, kept_high,
    load_sem, halo_send, halo_recv, one_send, one_recv, two_send, two_recv, two_low_send, two_low_recv, z_send, z_recv,
    run_send, run_recv, level_send, level_recv,
    own_one_send, own_one_recv, own_two_send, own_two_recv, own_z_send, own_z_recv,
    count_send, count_recv, kept_one_send, kept_one_recv, kept_two_send, kept_two_recv, kept_z_send, kept_z_recv,
):
    win = lax.axis_index("win")
    plane = lax.axis_index("pair")
    row = win // GROUP
    member = win % GROUP
    above = (win, (plane + 1) % RING)
    below = (win, (plane + RING - 1) % RING)
    has_above, has_below = plane < RING - 1, plane > 0
    sends_up, takes_low = plane < RING - 2, (plane > 0) & (plane < RING - 1)
    sends_down, takes_high = plane > 0, plane < RING - 1

    def in_group(step):
        return (row * GROUP + (member + step) % GROUP, plane)

    def in_ring(step):
        return (((row + step) % RING) * GROUP + member, plane)

    for ref in (count_low, count_high, kept_low, kept_high):
        ref[...] = jnp.ones_like(ref)
    for ref in (own_low, own_high, got_low, level_low, level_high):
        ref[...] = jnp.zeros_like(ref)

    barrier = pltpu.get_barrier_semaphore()

    @pl.when(has_above)
    def _():
        pl.semaphore_signal(barrier, inc=1, device_id=above, device_id_type=MESH)

    @pl.when(has_below)
    def _():
        pl.semaphore_signal(barrier, inc=1, device_id=below, device_id_type=MESH)

    for step in range(1, GROUP):
        pl.semaphore_signal(barrier, inc=1, device_id=in_group(step), device_id_type=MESH)
    for step in range(1, RING):
        pl.semaphore_signal(barrier, inc=1, device_id=in_ring(step), device_id_type=MESH)

    count_load = pltpu.make_async_copy(counts_hbm, counts, load_sem.at[0])
    pairs_load = pltpu.make_async_copy(pairs_hbm, pairs, load_sem.at[1])
    live_load = pltpu.make_async_copy(live_hbm, live, load_sem.at[2])
    turn_load = pltpu.make_async_copy(turns, turn_table, load_sem.at[3])
    place_load = pltpu.make_async_copy(places, place_table, load_sem.at[4])
    own_load = pltpu.make_async_copy(spectra.at[:, 0], own, load_sem.at[5])
    for load in (count_load, pairs_load, live_load, turn_load, place_load, own_load):
        load.start()
    count_load.wait()
    count_own[...] = jnp.full((8, 128), counts[0, 0].astype(jnp.float32))
    pl.semaphore_wait(barrier, GROUP - 1 + RING - 1 + has_above.astype(jnp.int32) + has_below.astype(jnp.int32))

    def remote(source, target, send, recv, device):
        return pltpu.make_async_remote_copy(
            src_ref=source, dst_ref=target, send_sem=send, recv_sem=recv, device_id=device, device_id_type=MESH
        )

    def whole(ref, send, recv):
        return remote(ref, ref, send, recv, above)

    def both_sides(up, low_ref, down, high_ref, send, recv):
        return (
            remote(up, low_ref, send.at[0], recv.at[0], above),
            remote(down, high_ref, send.at[1], recv.at[1], below),
        )

    def halo(index):
        block = spectra.at[:, 0, pl.ds(pl.multiple_of(index * ROWS, ROWS), ROWS), :]
        return both_sides(block, low.at[index], block, high.at[index], halo_send.at[index], halo_recv.at[index])

    def runs(run):
        copies = []
        for side in range(2):
            lanes = pl.ds(side * BINS + RUNS[run][0], RUNS[run][1] - RUNS[run][0])
            block = spectra.at[:, 0, pl.ds(LAST * ROWS, ROWS), lanes]
            copies.append(
                both_sides(
                    block, low.at[LAST, :, :, lanes], block, high.at[LAST, :, :, lanes],
                    run_send.at[run, side], run_recv.at[run, side],
                )
            )
        return copies

    def next_halo(index):
        within = index < LAST
        begin(halo(lax.rem(index, PARTS)), sends_up & within, sends_down & within)
        for run in range(len(RUNS)):
            for copies in runs(run):
                begin(copies, sends_up & (index == LAST + run), sends_down & (index == LAST + run))

    def begin(copies, up, down):
        pl.when(up)(copies[0].start)
        pl.when(down)(copies[1].start)

    def end_send(copies, up, down):
        pl.when(up)(copies[0].wait_send)
        pl.when(down)(copies[1].wait_send)

    def end_recv(copies, takes_low, takes_high):
        pl.when(takes_low)(copies[0].wait_recv)
        pl.when(takes_high)(copies[1].wait_recv)

    for index in range(AHEAD):
        begin(halo(index), sends_up, sends_down)
    count_copies = both_sides(count_own, count_low, count_own, count_high, count_send, count_recv)
    begin(count_copies, has_above, has_below)

    @pl.when(jnp.logical_not(takes_low))
    def _():
        low[...] = jnp.zeros_like(low)

    @pl.when(jnp.logical_not(takes_high))
    def _():
        high[...] = jnp.zeros_like(high)

    turn_load.wait()
    place_load.wait()
    line = lax.broadcasted_iota(jnp.int32, (16, 128), 0)
    odd = (line % 2) == 1
    sign_sin = jnp.where(line % 4 < 2, 1.0, -1.0)
    sign_cos = jnp.where((line % 4 == 0) | (line % 4 == 3), 1.0, -1.0)

    @pl.loop(0, BINS // 16, unroll=2)
    def _(block):
        rows = pl.ds(pl.multiple_of(block * 16, 16), 16)
        shifted = pl.ds(pl.multiple_of(block * 16 + BINS, 16), 16)
        cos = place_table[rows, 0:HALF]
        minus_sin = place_table[rows, HALF : 2 * HALF]
        turn_cos = jnp.broadcast_to(turn_table[rows, 0:1], (16, 128))
        turn_sin = jnp.broadcast_to(turn_table[rows, 1:2], (16, 128))
        for index in range(GROUP):
            table[index, rows, HALF : 2 * HALF] = cos.astype(jnp.bfloat16)
            table[index, shifted, HALF : 2 * HALF] = minus_sin.astype(jnp.bfloat16)
            table[index, rows, 0:HALF] = (jnp.where(odd, minus_sin, cos) * sign_cos).astype(jnp.bfloat16)
            table[index, shifted, 0:HALF] = (jnp.where(odd, cos, minus_sin) * sign_sin).astype(jnp.bfloat16)
            if index < GROUP - 1:
                cos, minus_sin = (
                    cos * turn_cos + minus_sin * turn_sin,
                    minus_sin * turn_cos - cos * turn_sin,
                )

    def level(read, rows):
        square = jnp.zeros((rows, 128), jnp.float32)
        for lane in range(0, 2 * BINS, 128):
            entry = read(slice(lane, lane + 128))
            square = square + entry * entry
        mean = jnp.sum(square, axis=1, keepdims=True) * (1.0 / (2 * BINS))
        return jnp.broadcast_to(inverse_root(mean + 1e-6), (rows, 128))

    own_load.wait()
    mine = count_own[...]
    mask_own = jnp.concatenate([jnp.where(mine > 1.5, 1.0, 0.0)] * 2, axis=0)

    @pl.loop(0, CHANNELS // 16)
    def _(block):
        here = pl.ds(pl.multiple_of(block * 16, 16), 16)
        levels = []
        for window in range(2):
            levels.append(level(lambda lanes: own[window, here, lanes], 16))
            own_level[window, here, :] = levels[window]
        for lane in range(0, BINS, 128):
            real, imag = slice(lane, lane + 128), slice(BINS + lane, BINS + lane + 128)
            powers = []
            for window in range(2):
                re, im = own[window, here, real] * levels[window], own[window, here, imag] * levels[window]
                powers.append(re * re + im * im)
            weight = jnp.broadcast_to(band[:, real], (16, 128))
            own_stack[here, real] = ((powers[0] + mask_own * powers[1]) * weight).astype(jnp.bfloat16)

    def own_piece(step):
        own_term[step] = lax.dot_general(
            own_stack[...],
            table[(member + step) % GROUP, 0:BINS],
            (((1,), (0,)), ((), ())),
            preferred_element_type=jnp.float32,
        )

    @pl.loop(1, GROUP)
    def _(step):
        own_piece(step)
        remote(own_term.at[step], own_got_one.at[step - 1], own_one_send, own_one_recv, in_group(step)).start()

    own_piece(0)

    last_level = own_level.at[:, pl.ds(LAST * ROWS, ROWS)]
    level_copies = both_sides(last_level, level_low, last_level, level_high, level_send, level_recv)
    begin(level_copies, sends_up, sends_down)

    end_recv(count_copies, has_below, has_above)
    end_send(count_copies, has_above, has_below)
    above_count = count_high[...]
    side = jnp.minimum(mine, above_count)
    across = jnp.minimum(count_low[...], above_count)
    row_line = lax.broadcasted_iota(jnp.int32, (8, 128), 0)
    kept[...] = jnp.where(row_line == 0, mine, jnp.where(row_line == 1, side, across))
    for step in range(1, GROUP):
        remote(kept, kept_one.at[step - 1], kept_one_send, kept_one_recv, in_group(step)).start()
    mask_side = jnp.where(side > 1.5, 1.0, 0.0)
    mask_across = jnp.where(across > 1.5, 1.0, 0.0)

    def readers_of(index):
        here = pl.ds(pl.multiple_of(index * ROWS, ROWS), ROWS)

        def reader(kind, window):
            if kind == 0:
                return lambda lanes: own[window, here, lanes]
            ref = low if kind == 1 else high
            return lambda lanes: ref[index, window, :, lanes]

        return {(kind, window): reader(kind, window) for kind in range(3) for window in range(2)}

    def products(readers, levels, begin_lane, end_lane, place=0):
        rows = slice(place * LINES, (place + 1) * LINES)
        for lane in range(begin_lane, end_lane, 128):
            real, imag = slice(lane, lane + 128), slice(BINS + lane, BINS + lane + 128)
            weight = jnp.broadcast_to(band[:, real], (ROWS, 128))
            re = {key: read(real) * levels[key] for key, read in readers.items()}
            im = {key: read(imag) * levels[key] for key, read in readers.items()}

            def cross(a, b, mask):
                parts = []
                for window in range(2):
                    ra, ia, rb, ib = re[a, window], im[a, window], re[b, window], im[b, window]
                    parts.append((ra * rb + ia * ib, ia * rb - ra * ib))
                return (
                    (parts[0][0] + mask * parts[1][0]) * weight,
                    (parts[0][1] + mask * parts[1][1]) * weight,
                )

            side_re, side_im = cross(0, 2, mask_side)
            across_re, across_im = cross(1, 2, mask_across)
            stack[rows, real] = jnp.concatenate([side_re, across_re], axis=0).astype(jnp.bfloat16)
            stack[rows, imag] = jnp.concatenate([side_im, across_im], axis=0).astype(jnp.bfloat16)

    def times_table(lines, step, rows):
        return lax.dot_general(
            stack[0:lines, rows],
            table[(member + step) % GROUP, rows],
            (((1,), (0,)), ((), ())),
            preferred_element_type=jnp.float32,
        )

    def lines_of(unit):
        return LINES if isinstance(unit, int) and unit >= PAIRS else 2 * LINES

    def send_piece(unit, step):
        lines = pl.ds(0, lines_of(unit))
        remote(
            term.at[unit, step, lines], got_one.at[unit, step - 1, lines],
            one_send.at[unit], one_recv.at[unit], in_group(step),
        ).start()

    def cross_spectra(index, place):
        end_recv(halo(index), takes_low, takes_high)
        next_halo(index + AHEAD)
        here = pl.ds(pl.multiple_of(index * ROWS, ROWS), ROWS)
        readers = readers_of(index)
        levels = {
            key: own_level[key[1], here, :] if key[0] == 0 else level(read, ROWS) for key, read in readers.items()
        }
        products(readers, levels, 0, BINS, place)

    def correlate(unit):
        lines = lines_of(unit)

        @pl.loop(1, GROUP)
        def _(count):
            step = far_first(count)
            term[unit, step, 0:lines] = times_table(lines, step, slice(0, 2 * BINS))
            send_piece(unit, step)

        term[unit, 0, 0:lines] = times_table(lines, 0, slice(0, 2 * BINS))

    def correlate_last():
        end_recv(level_copies, takes_low, takes_high)
        end_send(level_copies, sends_up, sends_down)
        readers = readers_of(LAST)
        levels = {}
        for window in range(2):
            levels[0, window] = own_level[window, LAST * ROWS : PARTS * ROWS, :]
            levels[1, window] = level_low[window]
            levels[2, window] = level_high[window]
        for run, (start, stop) in enumerate(RUNS):
            for copies in runs(run):
                end_recv(copies, takes_low, takes_high)
            products(readers, levels, start, stop)
            real, imag = slice(start, stop), slice(BINS + start, BINS + stop)

            def piece(step):
                value = times_table(LINES, step, real) + times_table(LINES, step, imag)
                term[UNITS - 1, step, 0:LINES] = value if run == 0 else term[UNITS - 1, step, 0:LINES] + value

            @pl.loop(1, GROUP)
            def _(count):
                step = far_first(count)
                piece(step)
                if run == len(RUNS) - 1:
                    send_piece(UNITS - 1, step)

            piece(0)

    def packed(groups, chip):
        lane = lax.broadcasted_iota(jnp.int32, groups[0].shape, 1)
        value = None
        for place in reversed(range(len(groups))):
            shift = ((place - chip) * SHARE) % 128
            moved = pltpu.roll(groups[place], shift, axis=1) if shift else groups[place]
            value = moved if value is None else jnp.where(lane < (place + 1) * SHARE, moved, value)
        return value

    def pieces_of(unit):
        return got_one.at[unit, :, pl.ds(0, lines_of(unit))]

    def add_group(unit, up=False):
        whole(pieces_of(unit), one_send.at[unit], one_recv.at[unit]).wait_recv()
        lines = lines_of(unit)
        for half in range(2):
            lanes = slice(half * HALF, (half + 1) * HALF)
            value = term[unit, 0, 0:lines, lanes]
            for step in range(GROUP - 1):
                value = value + got_one[unit, step, 0:lines, lanes]
            groups = [value[start : start + ROWS] for start in range(0, lines, ROWS)]
            for chip in range(RING // 2):
                pack[unit, half * (RING // 2) + chip] = packed(groups, chip)
        for step in FAR_FIRST:
            if up:
                pl.when(has_above)(piece_up(unit, step).start)
            remote(
                pack.at[unit, (row + step) % RING], got_two.at[unit, step - 1],
                two_send, two_recv.at[unit], in_ring(step),
            ).start()
        if up:
            pl.when(has_above)(piece_up(unit, 0).start)

    def piece_up(unit, step):
        target = (row + step) % RING
        return remote(
            pack.at[unit, target], got_two_low.at[unit - TAIL, step], two_low_send, two_low_recv.at[unit - TAIL],
            (target * GROUP + member, plane + 1),
        )

    def sum_ring(index):
        whole(got_two.at[index], two_send, two_recv.at[index]).wait_recv()
        value = pack[index, row]
        for step in range(RING - 1):
            value = value + got_two[index, step]
        total[index] = value

    def add_ring(index):
        sum_ring(index)
        pl.when(has_above)(remote(total.at[index], got_low.at[index], z_send, z_recv, above).start)

    def sum_low(index):
        whole(got_two_low.at[index - TAIL], two_low_send, two_low_recv.at[index - TAIL]).wait_recv()
        value = got_two_low[index - TAIL, 0]
        for step in range(1, RING):
            value = value + got_two_low[index - TAIL, step]
        got_low[index] = value

    def kept_copies():
        return both_sides(kept_all, kept_low, kept_all, kept_high, kept_z_send, kept_z_recv)

    def own_copies():
        return both_sides(own_total, own_low, own_total, own_high, own_z_send, own_z_recv)

    @pl.loop(0, PAIRS)
    def _(unit):
        cross_spectra(2 * unit, 0)
        cross_spectra(2 * unit + 1, 1)
        correlate(unit)

        @pl.when(unit >= 1)
        def _():
            add_group(unit - 1)

        @pl.when(unit >= 2)
        def _():
            add_ring(unit - 2)

        @pl.when(unit == 1)
        def _():
            whole(kept_one, kept_one_send, kept_one_recv).wait()
            value = kept[...]
            for step in range(GROUP - 1):
                value = value + kept_one[step]
            kept_part[...] = value
            whole(own_got_one, own_one_send, own_one_recv).wait()
            for half in range(2):
                lanes = slice(half * HALF, (half + 1) * HALF)
                groups = []
                for block in range(4):
                    rows = slice(block * 16, (block + 1) * 16)
                    value = own_term[0, rows, lanes]
                    for step in range(GROUP - 1):
                        value = value + own_got_one[step, rows, lanes]
                    groups.append(value)
                for chip in range(RING // 2):
                    own_pack[half * (RING // 2) + chip] = packed(groups, chip)
            for step in range(1, RING):
                remote(kept_part, kept_two.at[step - 1], kept_two_send, kept_two_recv, in_ring(step)).start()
                remote(
                    own_pack.at[(row + step) % RING], own_got_two.at[step - 1], own_two_send, own_two_recv, in_ring(step)
                ).start()

        @pl.when(unit == 2)
        def _():
            whole(kept_two, kept_two_send, kept_two_recv).wait()
            whole(own_got_two, own_two_send, own_two_recv).wait()
            value = kept_part[...]
            own_value = own_pack[row]
            for step in range(RING - 1):
                value = value + kept_two[step]
                own_value = own_value + own_got_two[step]
            kept_all[...] = value
            own_total[...] = own_value
            begin(kept_copies(), has_above, has_below)
            begin(own_copies(), has_above, has_below)

    cross_spectra(LAST - 1, 0)
    correlate(PAIRS)
    correlate_last()
    add_ring(TAIL - 1)
    add_group(TAIL, up=True)
    add_group(PAIRS, up=True)
    add_group(UNITS - 1, up=True)
    pairs_load.wait()
    live_load.wait()
    for copies in (kept_copies(), own_copies()):
        end_recv(copies, has_below, has_above)
        end_send(copies, has_above, has_below)
    for place, source in enumerate((own_low, own_total, own_high)):
        value = source[...]
        for block in range(4):
            rows = slice(block * 16, (block + 1) * 16)
            own_wide[place, rows, :] = pltpu.roll(value, 128 - block * SHARE, axis=1) if block else value

    kept_options = [
        kept_low[0:1], kept_low[1:2], kept_all[2:3], kept_all[0:1], kept_all[1:2], kept_high[0:1],
    ]

    def choose(slot, options):
        a, b = pairs[0, 0, slot], pairs[0, 1, slot]
        tests = [
            (a == plane - 1) & (b == plane),
            (a == plane - 1) & (b == plane + 1),
            (a == plane) & (b == plane),
            (a == plane) & (b == plane + 1),
            (a == plane + 1) & (b == plane + 1),
        ]
        value = options[0]
        for test, option in zip(tests, options[1:]):
            value = jnp.where(test, option, value)
        return value

    scales = []
    for slot in range(SLOTS):
        alive = (slot < live[0]).astype(jnp.float32)
        scales.append(jnp.broadcast_to(alive / choose(slot, kept_options), (ROWS, 128)))

    def fill(unit):
        for part in range(2 if unit < PAIRS else 1):
            index = 2 * unit + part if unit < PAIRS else LAST - UNITS + 1 + unit
            rows = slice(index * ROWS, (index + 1) * ROWS)
            lane = part * 2 * SHARE

            def side(tile):
                return pltpu.roll(tile, 128 - lane, axis=1) if lane else tile

            options = [
                own_wide[0, rows], side(got_low[unit]), pltpu.roll(total[unit], 128 - SHARE - lane, axis=1),
                own_wide[1, rows], side(total[unit]), own_wide[2, rows],
            ]
            for slot in range(SLOTS):
                start = slot * CHANNELS + index * ROWS
                chosen[start : start + ROWS, :] = choose(slot, options) * scales[slot]

    def settle(unit):
        sum_ring(unit)
        pl.when(has_below)(lambda: sum_low(unit))
        fill(unit)

    early = got_low.at[pl.ds(0, TAIL)]
    pl.when(has_below)(whole(early, z_send, z_recv).wait_recv)
    for unit in range(TAIL):
        fill(unit)
    pl.when(has_above)(whole(early, z_send, z_recv).wait_send)
    for unit in range(TAIL, UNITS - 1):
        settle(unit)
    for unit in range(UNITS):
        whole(pieces_of(unit), one_send.at[unit], one_recv.at[unit]).wait_send()
    for index in range(LAST):
        end_send(halo(index), sends_up, sends_down)
    for run in range(len(RUNS)):
        for copies in runs(run):
            end_send(copies, sends_up, sends_down)
    settle(UNITS - 1)
    for block in range(SLOTS * CHANNELS // 128):
        lanes = slice(block * 128, (block + 1) * 128)
        out[:, lanes] = chosen[lanes, :].T[:SHARE]
    whole(got_two, two_send, two_recv.at[0]).wait_send()
    pl.when(has_above)(whole(got_two_low, two_low_send, two_low_recv.at[0]).wait_send)


def on_device(spectra, counts, band_filter, pair_list, live_slots):
    turns, places = twiddles()
    f32, bf16, i32 = jnp.float32, jnp.bfloat16, jnp.int32
    dma = pltpu.SemaphoreType.DMA
    tile = (8, 128)
    vmem = pltpu.VMEM
    anywhere = pl.BlockSpec(memory_space=pl.ANY)
    far = pl.BlockSpec(memory_space=pltpu.HBM)
    return pl.pallas_call(
        kernel,
        out_shape=jax.ShapeDtypeStruct((SHARE, SLOTS * CHANNELS), f32),
        in_specs=[anywhere, far, pl.BlockSpec(memory_space=vmem), far, far, anywhere, anywhere],
        out_specs=pl.BlockSpec(memory_space=vmem),
        scratch_shapes=[
            pltpu.SMEM((1, 1), i32), pltpu.SMEM((1, 2, SLOTS), i32), pltpu.SMEM((1,), i32),
            vmem((2, CHANNELS, 2 * BINS), f32),
            vmem((2, CHANNELS, 128), f32),
            vmem((PARTS, 2, ROWS, 2 * BINS), f32),
            vmem((PARTS, 2, ROWS, 2 * BINS), f32),
            vmem((BINS, 128), f32),
            vmem((BINS, 2 * HALF), f32),
            vmem((GROUP, 2 * BINS, PIECE), bf16),
            vmem((CHANNELS, BINS), bf16),
            vmem((GROUP, CHANNELS, PIECE), f32),
            vmem((GROUP - 1, CHANNELS, PIECE), f32),
            vmem((RING, 16, 128), f32),
            vmem((RING - 1, 16, 128), f32),
            vmem((16, 128), f32), vmem((16, 128), f32), vmem((16, 128), f32),
            vmem((3, CHANNELS, 128), f32),
            vmem((2 * LINES, 2 * BINS), bf16),
            vmem((UNITS, GROUP, 2 * LINES, PIECE), f32),
            vmem((UNITS, GROUP - 1, 2 * LINES, PIECE), f32),
            vmem((UNITS, RING) + tile, f32),
            vmem((UNITS, RING - 1) + tile, f32),
            vmem((UNITS - TAIL, RING) + tile, f32),
            vmem((UNITS,) + tile, f32),
            vmem((UNITS,) + tile, f32),
            vmem((SLOTS * CHANNELS, 128), f32),
            vmem((2,) + tile, f32), vmem((2,) + tile, f32),
            vmem(tile, f32), vmem(tile, f32), vmem(tile, f32),
            vmem(tile, f32),
            vmem((GROUP - 1,) + tile, f32),
            vmem(tile, f32),
            vmem((RING - 1,) + tile, f32),
            vmem(tile, f32), vmem(tile, f32), vmem(tile, f32),
            dma((6,)),
            dma((PARTS, 2)), dma((PARTS, 2)),
            dma((UNITS,)), dma((UNITS,)),
            dma, dma((UNITS,)),
            dma, dma((UNITS - TAIL,)),
            dma, dma,
            dma((len(RUNS), 2, 2)), dma((len(RUNS), 2, 2)),
            dma((2,)), dma((2,)),
            dma, dma, dma, dma,
            dma((2,)), dma((2,)),
            dma((2,)), dma((2,)),
            dma, dma, dma, dma,
            dma((2,)), dma((2,)),
        ],
        compiler_params=pltpu.CompilerParams(
            collective_id=0, has_side_effects=True, vmem_limit_bytes=56 * 1024 * 1024
        ),
    )(
        spectra, counts, band_filter.reshape(1, BINS), jnp.swapaxes(pair_list, 1, 2), live_slots,
        jnp.asarray(turns), jnp.asarray(places),
    )


def solution(mesh):
    placed = (P("win", "pair", None, None), P("win", "pair"), P(), P("pair", None, None), P("pair"))
    return jax.shard_map(
        on_device, mesh=mesh, in_specs=placed, out_specs=P("win", "pair"), check_vma=False
    )
```
